512 devices in a mesh: stream: 32 (over x, y), azim: 16 (over z, core).
Axes of the slice: x: 4, y: 8, z: 8, core: 2. Of those that a mesh axis runs over, the one named last changes fastest.
Arguments:
- state_in: float32 [21, 1024, 32, 128], P(None, None, 'azim', 'stream'), may hold values from -6 to 6
- new_index: int32 [1024], P('stream'), may hold values from 0 to 1023, as said below
- stencil_index: int32 [1024, 32, 128], P('stream', 'azim'), may hold values from 0 to 126
- stencil_weight: float32 [1024, 32, 128], P('stream', 'azim'), may hold values from 0 to 1
- cell_count: int32 [1024, 32], P('stream', 'azim'), may hold values from 64 to 128
- normal_speed: float32 [1024, 32, 128], P('stream', 'azim'), may hold values from 0.2 to 0.9
- azim_diffusion: float32 [1024, 32, 128], P('stream', 'azim'), may hold values from 0.05 to 0.4
- mixing: float32 [21, 21], replicated, may hold values from -1.25 to 1.25
Outputs:
- state_out: float32 [21, 1024, 32, 128], P(None, 'stream', 'azim')
The draws below stay inside these ranges and needn't reach their ends.
Inputs may be any that keep to these rules, and one draw needn't show every extreme that they name: A permutation of the stations. The new owner of station s is new_index[s] // 32; one device's stations go to one owner at most 2 at a time, exactly 2 for some owners, and how many depends only on the difference of the two stream indices modulo 32.
All inputs are finite; a program needn't handle non-finite values.
Results may differ from the reference program's by a relative error of at most 0.000071.
Values sent between devices are 32-bit elements; how exact they have to be, the bound alone decides.
No kernel may reach another device: no remote copies, remote signals or barrier semaphores. Data moves between devices by JAX's collectives and lax.ppermute only.
A program may use at most 64 MiB of HBM per device.

```python
import math
import jax
import jax.numpy as jnp
from jax import lax

NV = 21
NN = 128
LS_DEV = 32
CAP = 2
LSTR = 1024
LAZ = 32
N_STREAM = 32


def draw_new_index(key, part):
    key = jax.random.fold_in(key, 7)
    key_rank, key_send, key_arrive = jax.random.split(key, 3)
    peer_total = N_STREAM
    rank_order = jax.random.permutation(key_rank, peer_total)
    ranks = jnp.arange(peer_total, dtype=jnp.int32)
    by_rank = jnp.where(ranks < peer_total // 4, CAP, jnp.where(ranks < 3 * peer_total // 4, CAP // 2, 0)).astype(jnp.int32)
    counts = jnp.zeros((peer_total,), jnp.int32).at[rank_order].set(by_rank)
    offsets = jnp.repeat(ranks, counts, total_repeat_length=LS_DEV)
    send_order = jax.vmap(lambda one_key: jax.random.permutation(one_key, LS_DEV))(jax.random.split(key_send, peer_total))
    arrive = jax.vmap(lambda one_key: jax.random.permutation(one_key, LS_DEV))(jax.random.split(key_arrive, peer_total))
    sender = ranks[:, None]
    receiver = (sender + offsets[send_order]) % peer_total
    arrival = arrive[receiver, send_order]
    return (receiver * LS_DEV + arrival).reshape(-1).astype(jnp.int32)


def touch_ends(drawn, rng, least, largest):
    dims = drawn.shape
    index_at = [jax.random.randint(jax.random.fold_in(rng, axis), (), 0, dims[axis]) for axis in range(len(dims))]
    drawn = drawn.at[tuple(index_at)].set(least)
    longest = dims.index(max(dims))
    index_at[longest] = (index_at[longest] + 1) % dims[longest]
    return drawn.at[tuple(index_at)].set(largest)


def steps_of(stream_key, shape, pieces, smallest, high):
    factor_of, own = 1.0, jax.random.fold_in(stream_key, 6)
    for axis_at, shards_of in pieces:
        heights = jnp.exp(jax.random.uniform(jax.random.fold_in(own, axis_at), (shards_of,), jnp.float32, smallest / len(pieces), high / len(pieces)))
        factor_of = factor_of * jnp.repeat(heights, shape[axis_at] // shards_of).reshape([-1 if axis == axis_at else 1 for axis in range(len(shape))])
    return factor_of


def gaussian(stream_key, dims, scale, most, cuts=(), kind=jnp.bfloat16):
    drawn = scale * jax.random.normal(stream_key, dims, jnp.float32)
    if cuts:
        drawn = drawn * steps_of(stream_key, dims, cuts, -0.22, 0.18)
    return jnp.clip(drawn, -most, most).astype(kind)


def setup_inputs(seed: int = 0) -> dict:
    key_list = jax.random.split(jax.random.key(seed), 9)
    state_in = gaussian(key_list[0], (NV, LSTR, LAZ, NN), 1.0, 6.0, ((2, 16), (3, 32)), jnp.float32)
    new_index = draw_new_index(jax.random.fold_in(key_list[8], 71), 0)
    stencil_index = touch_ends(jax.random.randint(key_list[2], (LSTR, LAZ, NN), 0, NN - 1), jax.random.fold_in(key_list[2], 1), 0, (NN - 1) - 1).astype(jnp.int32)
    stencil_weight = jnp.clip(1.0 * jax.random.uniform(key_list[3], (LSTR, LAZ, NN), jnp.float32) ** steps_of(key_list[3], (LSTR, LAZ, NN), ((0, 32), (1, 16)), -0.2, 0.2), 0.0, 1.0)
    cell_count = touch_ends(jax.random.randint(key_list[4], (LSTR, LAZ), NN // 2, NN + 1), jax.random.fold_in(key_list[4], 1), NN // 2, NN).astype(jnp.int32)
    normal_speed = jnp.clip(0.2 + 0.7 * jax.random.uniform(key_list[5], (LSTR, LAZ, NN), jnp.float32) ** steps_of(key_list[5], (LSTR, LAZ, NN), ((0, 32), (1, 16)), -0.2, 0.2), 0.2, 0.9)
    azim_diffusion = jnp.clip(jnp.exp(math.log(0.4) - 2.0794415 * jax.random.uniform(key_list[6], (LSTR, LAZ, NN), jnp.float32) ** steps_of(key_list[6], (LSTR, LAZ, NN), ((0, 32), (1, 16)), -0.2, 0.2)), 0.05, 0.4)
    mixing = gaussian(key_list[7], (NV, NV), NV ** -0.5, 1.25, (), jnp.float32)
    return dict(state_in=state_in, new_index=new_index, stencil_index=stencil_index, stencil_weight=stencil_weight, cell_count=cell_count, normal_speed=normal_speed, azim_diffusion=azim_diffusion, mixing=mixing)


def recluster(flow_state, stencil_index, stencil_weight, cell_count):
    lower_value = jnp.take_along_axis(flow_state, jnp.broadcast_to(stencil_index[None], flow_state.shape), axis=3)
    upper_value = jnp.take_along_axis(flow_state, jnp.broadcast_to(stencil_index[None] + 1, flow_state.shape), axis=3)
    weight = stencil_weight[None]
    fitted = (1.0 - weight) * lower_value + weight * upper_value
    active = active_mask(cell_count, flow_state.shape[3])
    return jnp.where(active[None] > 0.0, fitted, jnp.float32(0.0))


def active_mask(cell_count, cell_total):
    return (jnp.arange(cell_total, dtype=jnp.int32)[None, None, :] < cell_count[:, :, None]).astype(jnp.float32)


def flux_rate(widened, line_speed, diffuse, mixing):
    center = widened[:, :, 1:-1]
    below_cell = jnp.concatenate([jnp.zeros_like(center[..., :1]), center[..., :-1]], axis=3)
    lateral = (widened[:, :, 2:] + widened[:, :, :-2]) - 2.0 * center
    mixed_term = jnp.einsum("uv,vsan->usan", mixing, center, precision=lax.Precision.HIGHEST)
    return diffuse * lateral - line_speed * (center - below_cell) - 0.25 * mixed_term


def cycle_pad(current):
    return jnp.concatenate([current[:, :, -1:], current, current[:, :, :1]], axis=2)


def reference(state_in, new_index, stencil_index, stencil_weight, cell_count, normal_speed, azim_diffusion, mixing):
    fitted = recluster(state_in, stencil_index, stencil_weight, cell_count)
    active = active_mask(cell_count, state_in.shape[3])
    moved_state = jnp.zeros_like(fitted).at[:, new_index].set(fitted)
    moved_active = jnp.zeros_like(active).at[new_index].set(active)
    section_one = moved_state + moved_active * flux_rate(cycle_pad(moved_state), normal_speed, azim_diffusion, mixing)
    return 0.5 * ((moved_state + section_one) + moved_active * flux_rate(cycle_pad(section_one), normal_speed, azim_diffusion, mixing))
```

```python
import functools
import jax
import jax.numpy as jnp
from jax import lax
from jax.experimental import pallas as pl
from jax.experimental.pallas import tpu as pltpu
from jax.sharding import PartitionSpec as P

LANES = 128
SLOTS = 2
HIGHEST = lax.Precision.HIGHEST
F32 = jnp.float32
BF16 = jnp.bfloat16
I32 = jnp.int32


def call(body, outs, *args, flops=0):
    touched = sum(a.size * a.dtype.itemsize for a in args) + sum(
        4 * functools.reduce(lambda x, y: x * y, o.shape) for o in outs
    )
    return pl.pallas_call(
        body,
        out_shape=outs,
        in_specs=[pl.BlockSpec(memory_space=pltpu.VMEM)] * len(args),
        out_specs=[pl.BlockSpec(memory_space=pltpu.VMEM)] * len(outs),
        compiler_params=pltpu.CompilerParams(vmem_limit_bytes=24 * 2**20),
        cost_estimate=pl.CostEstimate(flops=flops, bytes_accessed=touched, transcendentals=0),
    )(*args)


def iota(shape, dim):
    return lax.broadcasted_iota(I32, shape, dim)


def split(x):
    high = x.astype(BF16).astype(F32)
    return high, x - high


def rows_of(slot, azim):
    return slot * 2 + azim


STENCIL_ROWS = 10


def stencil_pack(nid_ref, idx_ref, weight_ref, count_ref, out_ref):
    rows = STENCIL_ROWS
    stations = idx_ref.shape[0] // 2
    peers = out_ref.shape[0] // rows
    nid = nid_ref[:, :stations]
    target = nid // stations
    place = nid % stations
    owners = (iota((peers, stations), 0) == target).astype(F32)
    before = (iota((stations, stations), 0) < iota((stations, stations), 1)).astype(F32)
    earlier = jnp.dot(owners, before, preferred_element_type=F32)
    rank = jnp.sum(owners * earlier, axis=0, keepdims=True)
    lane = iota((peers, LANES), 1)
    places = jnp.full((peers, LANES), -1.0, F32)
    cell = iota((stations, LANES), 1)
    for slot in range(SLOTS):
        pick = jnp.where(rank == float(slot), owners, 0.0)
        found = jnp.sum(pick * (place + 1).astype(F32), axis=1, keepdims=True) - 1.0
        places = jnp.where(lane == slot, found, places)
        for azim in range(2):
            idx = idx_ref[pl.ds(azim, stations, stride=2), :]
            live = cell < count_ref[:, azim : azim + 1]
            idx = jnp.where(live, idx, -1).astype(F32)
            weight = weight_ref[pl.ds(azim, stations, stride=2), :]
            at = rows_of(slot, azim)
            out_ref[pl.ds(at, peers, stride=rows), :] = jnp.dot(
                pick, idx, preferred_element_type=F32
            )
            out_ref[pl.ds(4 + at, peers, stride=rows), :] = jnp.dot(
                pick, weight, preferred_element_type=F32, precision=HIGHEST
            )
    out_ref[pl.ds(8, peers, stride=rows), :] = jnp.broadcast_to(
        nid_ref[...].astype(F32), (peers, LANES)
    )
    out_ref[pl.ds(9, peers, stride=rows), :] = places


STATE_ROWS = 44


def state_pack(got_ref, x_ref, out_ref):
    rows, stencil_rows = STATE_ROWS, STENCIL_ROWS
    peers = out_ref.shape[0] // rows
    total = x_ref.shape[1]
    new_rows = got_ref[pl.ds(8, peers, stride=stencil_rows), :].astype(I32)
    quarter = iota((1, LANES), 1) // 32
    tiles = []
    for tile in range(total // LANES):
        row = new_rows[4 * tile : 4 * tile + 1]
        for i in range(1, 4):
            row = jnp.where(quarter == i, new_rows[4 * tile + i : 4 * tile + i + 1], row)
        tiles.append(row)
    nid = jnp.concatenate(tiles, axis=1)
    high, low = split(x_ref[...])
    both = jnp.concatenate([high, low], axis=0).astype(BF16)
    lines = x_ref.shape[0]
    width = 2 * LANES
    for chunk in range(total // width):
        pick = jnp.where(iota((width, total), 0) + chunk * width == nid, 1.0, 0.0).astype(BF16)
        moved = lax.dot_general(
            both, pick, (((1,), (1,)), ((), ())), preferred_element_type=F32
        )
        moved = moved[:lines] + moved[lines:]
        for tile in range(2):
            y = moved[:, tile * LANES : (tile + 1) * LANES]
            first = (chunk * 2 + tile) * 4
            for group in range(5):
                part = [y[(4 * group + i) * 8 : (4 * group + i + 1) * 8] for i in range(4)]
                turned = []
                for d in range(4):
                    diag = part[d]
                    for q in range(1, 4):
                        diag = jnp.where(quarter == q, part[(q + d) % 4], diag)
                    turned.append(diag if d == 0 else pltpu.roll(diag, 32 * d, 1))
                for q in range(4):
                    out = turned[(-q) % 4]
                    for i in range(1, 4):
                        out = jnp.where(quarter == i, turned[(i - q) % 4], out)
                    at = (first + q) * rows + 8 * group
                    out_ref[at : at + 8, :] = out
            rest = y[160:168]
            turned = [rest] + [pltpu.roll(rest, 32 * d, 1) for d in range(1, 4)]
            for q in range(4):
                out = jnp.where(quarter == 0, turned[(-q) % 4][:4], turned[(1 - q) % 4][4:])
                at = (first + q) * rows + 40
                out_ref[at : at + 4, :] = out


def stencil_place(got_ref, speed_ref, diffuse_ref, low_ref, up_ref, wl_ref, wu_ref, lines_ref):
    rows = STENCIL_ROWS
    peers = got_ref.shape[0] // rows
    stations = low_ref.shape[0] // 2
    spots = got_ref[pl.ds(9, peers, stride=rows), :].T
    place = iota((stations, peers), 0).astype(F32)
    picks = [jnp.where(spots[slot : slot + 1, :] == place, 1.0, 0.0) for slot in range(SLOTS)]
    for azim in range(2):
        idx = jnp.zeros((stations, LANES), F32)
        weight = jnp.zeros((stations, LANES), F32)
        for slot in range(SLOTS):
            at = rows_of(slot, azim)
            idx += jnp.dot(
                picks[slot],
                got_ref[pl.ds(at, peers, stride=rows), :],
                preferred_element_type=F32,
            )
            weight += jnp.dot(
                picks[slot],
                got_ref[pl.ds(4 + at, peers, stride=rows), :],
                preferred_element_type=F32,
                precision=HIGHEST,
            )
        live = idx >= 0.0
        low = jnp.where(live, idx, 0.0).astype(I32)
        up = low + 1
        here = pl.ds(azim * stations, stations)
        low_ref[here, :] = (low % 4) * 32 + low // 4
        up_ref[here, :] = (up % 4) * 32 + up // 4
        wl_ref[here, :] = jnp.where(live, 1.0 - weight, 0.0)
        wu_ref[here, :] = jnp.where(live, weight, 0.0)
        lines_ref[pl.ds(azim * stations, stations), :] = speed_ref[
            pl.ds(azim, stations, stride=2), :
        ]
        lines_ref[pl.ds((2 + azim) * stations, stations), :] = diffuse_ref[
            pl.ds(azim, stations, stride=2), :
        ]
        lines_ref[pl.ds((4 + azim) * stations, stations), :] = jnp.where(live, 1.0, 0.0)


def refit(got_ref, low_ref, up_ref, wl_ref, wu_ref, out_ref):
    rows = STATE_ROWS
    stations = low_ref.shape[0] // 2

    def lines(first_row):
        cells = [
            got_ref[pl.ds(block * 8 * rows + first_row + c, 8, stride=rows), :]
            for c in range(4)
            for block in range(4)
        ]
        return jnp.concatenate(cells, axis=0).T

    def fit(x, azim, line):
        here = pl.ds(azim * stations, stations)
        lower = jnp.take_along_axis(x, low_ref[here, :], axis=1)
        upper = jnp.take_along_axis(x, up_ref[here, :], axis=1)
        out_ref[pl.ds(line * stations, stations), :] = (
            wl_ref[here, :] * lower + wu_ref[here, :] * upper
        )

    for group in range(5):
        for half in range(2):
            x = lines(8 * group + 4 * half)
            for i in range(4):
                fit(x[i * stations : (i + 1) * stations], half, 8 * group + 2 * i + half)
    x = lines(40)
    for half in range(2):
        fit(x[half * stations : (half + 1) * stations], half, 40 + half)


def sections(m_ref, left_ref, right_ref, lines_ref, lines_left_ref, lines_right_ref, mix_ref, out_ref):
    nv = m_ref.shape[0]
    stations = m_ref.shape[1] // 2
    cell = iota((nv, 8, LANES), 2)
    mix = mix_ref[...]

    def mixed(fields):
        x = jnp.concatenate([f.reshape(nv * 8, LANES) for f in fields], axis=1)
        high, low = split(x)
        pad = jnp.zeros((8, x.shape[1]), F32)
        stacked = jnp.concatenate([high, low, high, pad], axis=0).astype(BF16)
        y = jnp.dot(mix, stacked, preferred_element_type=F32)[: nv * 8]
        return [
            y[:, i * LANES : (i + 1) * LANES].reshape(nv, 8, LANES) for i in range(len(fields))
        ]

    def rate(below, center, above, term, speed, diffuse):
        lateral = (above + below) - 2.0 * center
        shifted = jnp.where(cell == 0, 0.0, pltpu.roll(center, 1, 2))
        return diffuse * lateral - speed * (center - shifted) - term

    def coefficients(ref, azim, block):
        def one(kind):
            return ref[pl.ds((2 * kind + azim) * stations + 8 * block, 8), :][None]

        return one(0), one(1), one(2)

    for block in range(stations // 8):
        def line(ref, azim):
            return ref[:, pl.ds(azim * stations + 8 * block, 8), :]

        field = [line(r, a) for r in (left_ref, m_ref, right_ref) for a in range(2)]
        co = [
            coefficients(lines_left_ref, 1, block),
            coefficients(lines_ref, 0, block),
            coefficients(lines_ref, 1, block),
            coefficients(lines_right_ref, 0, block),
        ]
        term = mixed(field[1:5])
        first = []
        for i in range(4):
            speed, diffuse, active = co[i]
            r = rate(field[i], field[i + 1], field[i + 2], term[i], speed, diffuse)
            first.append(field[i + 1] + active * r)
        term = mixed(first[1:3])
        for azim in range(2):
            speed, diffuse, active = co[1 + azim]
            r = rate(first[azim], first[azim + 1], first[azim + 2], term[azim], speed, diffuse)
            out = 0.5 * ((field[2 + azim] + first[1 + azim]) + active * r)
            out_ref[:, pl.ds(azim + 16 * block, 8, stride=2), :] = out


def shards(
    state_in,
    new_index,
    stencil_index,
    stencil_weight,
    cell_count,
    normal_speed,
    azim_diffusion,
    mixing,
):
    peers = lax.axis_size("stream")
    count = lax.axis_size("azim")
    nv, total, _, cells = state_in.shape
    stations = new_index.shape[0]
    shape = jax.ShapeDtypeStruct

    def flat(a):
        return a.reshape(2 * stations, LANES)

    def exchange(a):
        return lax.all_to_all(a, "stream", split_axis=0, concat_axis=0, tiled=True)

    def neighbours(a):
        up = [(i, (i + 1) % count) for i in range(count)]
        down = [((i + 1) % count, i) for i in range(count)]
        return lax.ppermute(a, "azim", up), lax.ppermute(a, "azim", down)

    (packed,) = call(
        stencil_pack,
        [shape((peers * STENCIL_ROWS, LANES), F32)],
        jnp.tile(new_index, LANES // stations)[None],
        flat(stencil_index),
        flat(stencil_weight),
        cell_count,
    )
    got = exchange(packed)

    x = state_in.transpose(0, 2, 3, 1).reshape(nv * 2 * cells, total)
    (packed,) = call(state_pack, [shape((peers * STATE_ROWS, LANES), F32)], got, x)
    got_state = exchange(packed)

    plane = shape((2 * stations, LANES), F32)
    index_plane = shape((2 * stations, LANES), I32)
    low, up, wl, wu, lines = call(
        stencil_place,
        [index_plane, index_plane, plane, plane, shape((6 * stations, LANES), F32)],
        got,
        flat(normal_speed),
        flat(azim_diffusion),
    )
    lines_left, lines_right = neighbours(lines)

    (moved,) = call(
        refit, [shape((nv * 2 * stations, LANES), F32)], got_state, low, up, wl, wu
    )
    left, right = neighbours(moved)

    mix = 0.25 * mixing
    high = lax.reduce_precision(mix, 8, 7)
    eye = jnp.eye(8, dtype=F32)

    def spread(a):
        return (a[:, None, :, None] * eye[None, :, None, :]).reshape(nv * 8, nv * 8)

    wide = jnp.concatenate([spread(high), spread(high), spread(mix - high)], axis=1)
    wide = jnp.pad(wide, ((0, 8), (0, 8))).astype(BF16)
    field = (nv, 2 * stations, LANES)
    (out,) = call(
        sections,
        [shape(field, F32)],
        moved.reshape(field),
        left.reshape(field),
        right.reshape(field),
        lines,
        lines_left,
        lines_right,
        wide,
    )
    return out.reshape(nv, stations, 2, LANES)


def solution(mesh):
    in_specs = (
        P(None, None, "azim", "stream"),
        P("stream"),
        P("stream", "azim", None),
        P("stream", "azim", None),
        P("stream", "azim"),
        P("stream", "azim", None),
        P("stream", "azim", None),
        P(),
    )
    out_specs = P(None, "stream", "azim", None)
    return jax.shard_map(shards, mesh=mesh, in_specs=in_specs, out_specs=out_specs, check_vma=False)
```

```python
import functools
import jax
import jax.numpy as jnp
from jax import lax
from jax.experimental import pallas as pl
from jax.experimental.pallas import tpu as pltpu
from jax.sharding import PartitionSpec as P

LANES = 128
SLOTS = 2
HIGHEST = lax.Precision.HIGHEST
F32 = jnp.float32
BF16 = jnp.bfloat16
I32 = jnp.int32


def call(body, outs, *args, flops=0, space=pltpu.VMEM, scratch=()):
    touched = sum(a.size * a.dtype.itemsize for a in args) + sum(
        4 * functools.reduce(lambda x, y: x * y, o.shape) for o in outs
    )
    return pl.pallas_call(
        body,
        out_shape=outs,
        in_specs=[pl.BlockSpec(memory_space=space)] * len(args),
        out_specs=[pl.BlockSpec(memory_space=pltpu.VMEM)] * len(outs),
        scratch_shapes=list(scratch),
        compiler_params=pltpu.CompilerParams(vmem_limit_bytes=24 * 2**20),
        cost_estimate=pl.CostEstimate(flops=flops, bytes_accessed=touched, transcendentals=0),
    )(*args)


def iota(shape, dim):
    return lax.broadcasted_iota(I32, shape, dim)


def split(x):
    high = x.astype(BF16).astype(F32)
    return high, x - high


def rows_of(slot, azim):
    return slot * 2 + azim


STENCIL_ROWS = 10


def stencil_pack(nid_hbm, idx_hbm, weight_hbm, count_hbm, out_ref, nid_ref, idx_ref, weight_ref, count_ref, sems):
    pairs = [(nid_hbm, nid_ref), (count_hbm, count_ref), (idx_hbm, idx_ref), (weight_hbm, weight_ref)]
    copies = [pltpu.make_async_copy(a, b, sems.at[i]) for i, (a, b) in enumerate(pairs)]
    for copy in copies:
        copy.start()
    for copy in copies:
        copy.wait()
    rows = STENCIL_ROWS
    stations = idx_ref.shape[0] // 2
    peers = out_ref.shape[0] // rows
    nid = nid_ref[...]
    target = nid // stations
    place = nid % stations
    owners = (iota((peers, stations), 0) == target).astype(F32)
    before = (iota((stations, stations), 0) < iota((stations, stations), 1)).astype(F32)
    earlier = jnp.dot(owners, before, preferred_element_type=F32)
    rank = jnp.sum(owners * earlier, axis=0, keepdims=True)
    same = iota((stations, stations), 0) == iota((stations, stations), 1)
    spread = (iota((stations, LANES), 1) % stations == iota((stations, LANES), 0)).astype(F32)
    wide = jnp.dot(
        jnp.broadcast_to(nid.astype(F32), (peers, stations)),
        spread,
        preferred_element_type=F32,
        precision=HIGHEST,
    )
    lane = iota((peers, LANES), 1)
    places = jnp.full((peers, LANES), -1.0, F32)
    cell = iota((stations, LANES), 1)
    counts = [
        jnp.sum(jnp.where(same, count_ref[azim : azim + 1, :], 0), axis=1, keepdims=True)
        for azim in range(2)
    ]
    for slot in range(SLOTS):
        pick = jnp.where(rank == float(slot), owners, 0.0)
        found = jnp.sum(pick * (place + 1).astype(F32), axis=1, keepdims=True) - 1.0
        places = jnp.where(lane == slot, found, places)
        for azim in range(2):
            idx = idx_ref[pl.ds(azim, stations, stride=2), :]
            live = cell < counts[azim]
            idx = jnp.where(live, idx, -1).astype(F32)
            weight = weight_ref[pl.ds(azim, stations, stride=2), :]
            at = rows_of(slot, azim)
            out_ref[pl.ds(at, peers, stride=rows), :] = jnp.dot(
                pick, idx, preferred_element_type=F32
            )
            out_ref[pl.ds(4 + at, peers, stride=rows), :] = jnp.dot(
                pick, weight, preferred_element_type=F32, precision=HIGHEST
            )
    out_ref[pl.ds(8, peers, stride=rows), :] = wide
    out_ref[pl.ds(9, peers, stride=rows), :] = places


STATE_ROWS = 44


def state_pack(got_ref, x_ref, out_ref):
    rows, stencil_rows = STATE_ROWS, STENCIL_ROWS
    peers = out_ref.shape[0] // rows
    total = x_ref.shape[1]
    new_rows = got_ref[pl.ds(8, peers, stride=stencil_rows), :].astype(I32)
    quarter = iota((1, LANES), 1) // 32
    tiles = []
    for tile in range(total // LANES):
        row = new_rows[4 * tile : 4 * tile + 1]
        for i in range(1, 4):
            row = jnp.where(quarter == i, new_rows[4 * tile + i : 4 * tile + i + 1], row)
        tiles.append(row)
    nid = jnp.concatenate(tiles, axis=1)
    high, low = split(x_ref[...])
    both = jnp.concatenate([high, low], axis=0).astype(BF16)
    lines = x_ref.shape[0]
    width = 2 * LANES
    for chunk in range(total // width):
        pick = jnp.where(iota((width, total), 0) + chunk * width == nid, 1.0, 0.0).astype(BF16)
        moved = lax.dot_general(
            both, pick, (((1,), (1,)), ((), ())), preferred_element_type=F32
        )
        moved = moved[:lines] + moved[lines:]
        for tile in range(2):
            y = moved[:, tile * LANES : (tile + 1) * LANES]
            first = (chunk * 2 + tile) * 4
            for group in range(5):
                part = [y[(4 * group + i) * 8 : (4 * group + i + 1) * 8] for i in range(4)]
                turned = []
                for d in range(4):
                    diag = part[d]
                    for q in range(1, 4):
                        diag = jnp.where(quarter == q, part[(q + d) % 4], diag)
                    turned.append(diag if d == 0 else pltpu.roll(diag, 32 * d, 1))
                for q in range(4):
                    out = turned[(-q) % 4]
                    for i in range(1, 4):
                        out = jnp.where(quarter == i, turned[(i - q) % 4], out)
                    at = (first + q) * rows + 8 * group
                    out_ref[at : at + 8, :] = out
            rest = y[160:168]
            turned = [rest] + [pltpu.roll(rest, 32 * d, 1) for d in range(1, 4)]
            for q in range(4):
                out = jnp.where(quarter == 0, turned[(-q) % 4][:4], turned[(1 - q) % 4][4:])
                at = (first + q) * rows + 40
                out_ref[at : at + 4, :] = out


def stencil_place(
    got_ref, speed_ref, diffuse_ref, mixing_ref, low_ref, up_ref, wl_ref, wu_ref, lines_ref, mix_ref
):
    nv = mixing_ref.shape[0]
    high, low = split(0.25 * mixing_ref[...])
    by_row = (iota((mix_ref.shape[0], nv), 0) // 8 == iota((mix_ref.shape[0], nv), 1)).astype(F32)
    by_column = (iota((nv, 8 * nv), 0) == iota((nv, 8 * nv), 1) // 8).astype(F32)
    both = [
        jnp.dot(
            jnp.dot(by_row, part, preferred_element_type=F32),
            by_column,
            preferred_element_type=F32,
        )
        for part in (high, low)
    ]
    same = iota(both[0].shape, 0) % 8 == iota(both[0].shape, 1) % 8
    both = [jnp.where(same, part, 0.0) for part in both]
    rest = jnp.zeros((mix_ref.shape[0], mix_ref.shape[1] - 24 * nv), F32)
    mix_ref[...] = jnp.concatenate([both[0], both[0], both[1], rest], axis=1).astype(BF16)
    rows = STENCIL_ROWS
    peers = got_ref.shape[0] // rows
    stations = low_ref.shape[0] // 2
    spots = got_ref[pl.ds(9, peers, stride=rows), :].T
    place = iota((stations, peers), 0).astype(F32)
    picks = [jnp.where(spots[slot : slot + 1, :] == place, 1.0, 0.0) for slot in range(SLOTS)]
    for azim in range(2):
        idx = jnp.zeros((stations, LANES), F32)
        weight = jnp.zeros((stations, LANES), F32)
        for slot in range(SLOTS):
            at = rows_of(slot, azim)
            idx += jnp.dot(
                picks[slot],
                got_ref[pl.ds(at, peers, stride=rows), :],
                preferred_element_type=F32,
            )
            weight += jnp.dot(
                picks[slot],
                got_ref[pl.ds(4 + at, peers, stride=rows), :],
                preferred_element_type=F32,
                precision=HIGHEST,
            )
        live = idx >= 0.0
        low = jnp.where(live, idx, 0.0).astype(I32)
        up = low + 1
        here = pl.ds(azim * stations, stations)
        low_ref[here, :] = (low % 4) * 32 + low // 4
        up_ref[here, :] = (up % 4) * 32 + up // 4
        wl_ref[here, :] = jnp.where(live, 1.0 - weight, 0.0)
        wu_ref[here, :] = jnp.where(live, weight, 0.0)
        lines_ref[pl.ds(azim * stations, stations), :] = speed_ref[
            pl.ds(azim, stations, stride=2), :
        ]
        lines_ref[pl.ds((2 + azim) * stations, stations), :] = diffuse_ref[
            pl.ds(azim, stations, stride=2), :
        ]
        lines_ref[pl.ds((4 + azim) * stations, stations), :] = jnp.where(live, 1.0, 0.0)


def refit(got_ref, low_ref, up_ref, wl_ref, wu_ref, out_ref):
    rows = STATE_ROWS
    stations = low_ref.shape[0] // 2

    def lines(first_row):
        cells = [
            got_ref[pl.ds(block * 8 * rows + first_row + c, 8, stride=rows), :]
            for c in range(4)
            for block in range(4)
        ]
        return jnp.concatenate(cells, axis=0).T

    def fit(x, azim, line):
        here = pl.ds(azim * stations, stations)
        lower = jnp.take_along_axis(x, low_ref[here, :], axis=1)
        upper = jnp.take_along_axis(x, up_ref[here, :], axis=1)
        out_ref[pl.ds(line * stations, stations), :] = (
            wl_ref[here, :] * lower + wu_ref[here, :] * upper
        )

    for group in range(5):
        for half in range(2):
            x = lines(8 * group + 4 * half)
            for i in range(4):
                fit(x[i * stations : (i + 1) * stations], half, 8 * group + 2 * i + half)
    x = lines(40)
    for half in range(2):
        fit(x[half * stations : (half + 1) * stations], half, 40 + half)


def sections(m_ref, left_ref, right_ref, lines_ref, lines_left_ref, lines_right_ref, mix_ref, out_ref):
    nv = m_ref.shape[0]
    stations = m_ref.shape[1] // 2
    cell = iota((nv, 8, LANES), 2)
    mix = mix_ref[...]

    def mixed(fields):
        x = jnp.concatenate([f.reshape(nv * 8, LANES) for f in fields], axis=1)
        high, low = split(x)
        pad = jnp.zeros((8, x.shape[1]), F32)
        stacked = jnp.concatenate([high, low, high, pad], axis=0).astype(BF16)
        y = jnp.dot(mix, stacked, preferred_element_type=F32)[: nv * 8]
        return [
            y[:, i * LANES : (i + 1) * LANES].reshape(nv, 8, LANES) for i in range(len(fields))
        ]

    def rate(below, center, above, term, speed, diffuse):
        lateral = (above + below) - 2.0 * center
        shifted = jnp.where(cell == 0, 0.0, pltpu.roll(center, 1, 2))
        return diffuse * lateral - speed * (center - shifted) - term

    def coefficients(ref, azim, block):
        def one(kind):
            return ref[pl.ds((2 * kind + azim) * stations + 8 * block, 8), :][None]

        return one(0), one(1), one(2)

    for block in range(stations // 8):
        def line(ref, azim):
            return ref[:, pl.ds(azim * stations + 8 * block, 8), :]

        field = [line(r, a) for r in (left_ref, m_ref, right_ref) for a in range(2)]
        co = [
            coefficients(lines_left_ref, 1, block),
            coefficients(lines_ref, 0, block),
            coefficients(lines_ref, 1, block),
            coefficients(lines_right_ref, 0, block),
        ]
        term = mixed(field[1:5])
        first = []
        for i in range(4):
            speed, diffuse, active = co[i]
            r = rate(field[i], field[i + 1], field[i + 2], term[i], speed, diffuse)
            first.append(field[i + 1] + active * r)
        term = mixed(first[1:3])
        for azim in range(2):
            speed, diffuse, active = co[1 + azim]
            r = rate(first[azim], first[azim + 1], first[azim + 2], term[azim], speed, diffuse)
            out = 0.5 * ((field[2 + azim] + first[1 + azim]) + active * r)
            out_ref[:, pl.ds(azim + 16 * block, 8, stride=2), :] = out


def shards(
    state_in,
    new_index,
    stencil_index,
    stencil_weight,
    cell_count,
    normal_speed,
    azim_diffusion,
    mixing,
):
    peers = lax.axis_size("stream")
    count = lax.axis_size("azim")
    nv, total, _, cells = state_in.shape
    stations = new_index.shape[0]
    shape = jax.ShapeDtypeStruct

    def flat(a):
        return a.reshape(2 * stations, LANES)

    def exchange(a, rows, tile):
        parts = a.reshape(peers, rows // tile, tile, LANES)
        parts = lax.all_to_all(parts, "stream", split_axis=0, concat_axis=0, tiled=True)
        return parts.reshape(peers * rows, LANES)

    def neighbours(a):
        up = [(i, (i + 1) % count) for i in range(count)]
        down = [((i + 1) % count, i) for i in range(count)]
        return lax.ppermute(a, "azim", up), lax.ppermute(a, "azim", down)

    (packed,) = call(
        stencil_pack,
        [shape((peers * STENCIL_ROWS, LANES), F32)],
        new_index[None],
        flat(stencil_index),
        flat(stencil_weight),
        cell_count.T,
        space=pltpu.HBM,
        scratch=[
            pltpu.VMEM((1, stations), I32),
            pltpu.VMEM((2 * stations, LANES), I32),
            pltpu.VMEM((2 * stations, LANES), F32),
            pltpu.VMEM((2, stations), I32),
            pltpu.SemaphoreType.DMA((4,)),
        ],
    )
    got = exchange(packed, STENCIL_ROWS, 2)

    x = state_in.transpose(0, 2, 3, 1).reshape(nv * 2 * cells, total)
    (packed,) = call(state_pack, [shape((peers * STATE_ROWS, LANES), F32)], got, x)
    got_state = exchange(packed, STATE_ROWS, 4)

    plane = shape((2 * stations, LANES), F32)
    index_plane = shape((2 * stations, LANES), I32)
    low, up, wl, wu, lines, mix = call(
        stencil_place,
        [
            index_plane,
            index_plane,
            plane,
            plane,
            shape((6 * stations, LANES), F32),
            shape((8 * nv + 8, 24 * nv + 8), BF16),
        ],
        got,
        flat(normal_speed),
        flat(azim_diffusion),
        mixing,
    )
    lines_left, lines_right = neighbours(lines)
    got_state, lines_left, lines_right = lax.optimization_barrier(
        (got_state, lines_left, lines_right)
    )

    (moved,) = call(
        refit, [shape((nv * 2 * stations, LANES), F32)], got_state, low, up, wl, wu
    )
    left, right = neighbours(moved)

    field = (nv, 2 * stations, LANES)
    (out,) = call(
        sections,
        [shape(field, F32)],
        moved.reshape(field),
        left.reshape(field),
        right.reshape(field),
        lines,
        lines_left,
        lines_right,
        mix,
    )
    return out.reshape(nv, stations, 2, LANES)


def solution(mesh):
    in_specs = (
        P(None, None, "azim", "stream"),
        P("stream"),
        P("stream", "azim", None),
        P("stream", "azim", None),
        P("stream", "azim"),
        P("stream", "azim", None),
        P("stream", "azim", None),
        P(),
    )
    out_specs = P(None, "stream", "azim", None)
    return jax.shard_map(shards, mesh=mesh, in_specs=in_specs, out_specs=out_specs, check_vma=False)
```

```python
import functools
import jax
import jax.numpy as jnp
from jax import lax
from jax.experimental import pallas as pl
from jax.experimental.pallas import tpu as pltpu
from jax.sharding import PartitionSpec as P

LANES = 128
SLOTS = 2
HIGHEST = lax.Precision.HIGHEST
F32 = jnp.float32
BF16 = jnp.bfloat16
I32 = jnp.int32


def call(body, outs, *args, space=pltpu.VMEM, out_space=pltpu.VMEM, scratch=(), room=24):
    touched = sum(a.size * a.dtype.itemsize for a in args) + sum(
        o.dtype.itemsize * functools.reduce(lambda x, y: x * y, o.shape) for o in outs
    )
    return pl.pallas_call(
        body,
        out_shape=outs,
        in_specs=[pl.BlockSpec(memory_space=space)] * len(args),
        out_specs=[pl.BlockSpec(memory_space=out_space)] * len(outs),
        scratch_shapes=list(scratch),
        compiler_params=pltpu.CompilerParams(vmem_limit_bytes=room * 2**20),
        cost_estimate=pl.CostEstimate(flops=0, bytes_accessed=touched, transcendentals=0),
    )(*args)


def iota(shape, dim):
    return lax.broadcasted_iota(I32, shape, dim)


def split(x):
    high = x.astype(BF16).astype(F32)
    return high, x - high


def rows_of(slot, azim):
    return slot * 2 + azim


STENCIL_ROWS = 10


def stencil_pack(nid_hbm, idx_hbm, weight_hbm, count_hbm, out_ref, nid_ref, idx_ref, weight_ref, count_ref, sems):
    pairs = [(nid_hbm, nid_ref), (count_hbm, count_ref), (idx_hbm, idx_ref), (weight_hbm, weight_ref)]
    copies = [pltpu.make_async_copy(a, b, sems.at[i]) for i, (a, b) in enumerate(pairs)]
    for copy in copies:
        copy.start()
    for copy in copies:
        copy.wait()
    rows = STENCIL_ROWS
    stations = idx_ref.shape[0] // 2
    peers = out_ref.shape[0] // rows
    nid = nid_ref[...]
    target = nid // stations
    place = nid % stations
    owners = (iota((peers, stations), 0) == target).astype(F32)
    before = (iota((stations, stations), 0) < iota((stations, stations), 1)).astype(F32)
    earlier = jnp.dot(owners, before, preferred_element_type=F32)
    rank = jnp.sum(owners * earlier, axis=0, keepdims=True)
    same = iota((stations, stations), 0) == iota((stations, stations), 1)
    spread = (iota((stations, LANES), 1) % stations == iota((stations, LANES), 0)).astype(F32)
    wide = jnp.dot(
        jnp.broadcast_to(nid.astype(F32), (peers, stations)),
        spread,
        preferred_element_type=F32,
        precision=HIGHEST,
    )
    lane = iota((peers, LANES), 1)
    places = jnp.full((peers, LANES), -1.0, F32)
    cell = iota((stations, LANES), 1)
    counts = [
        jnp.sum(jnp.where(same, count_ref[azim : azim + 1, :], 0), axis=1, keepdims=True)
        for azim in range(2)
    ]
    for slot in range(SLOTS):
        pick = jnp.where(rank == float(slot), owners, 0.0)
        found = jnp.sum(pick * (place + 1).astype(F32), axis=1, keepdims=True) - 1.0
        places = jnp.where(lane == slot, found, places)
        for azim in range(2):
            idx = idx_ref[pl.ds(azim, stations, stride=2), :]
            live = cell < counts[azim]
            idx = jnp.where(live, idx, -1).astype(F32)
            weight = weight_ref[pl.ds(azim, stations, stride=2), :]
            at = rows_of(slot, azim)
            out_ref[pl.ds(at, peers, stride=rows), :] = jnp.dot(
                pick, idx, preferred_element_type=F32
            )
            out_ref[pl.ds(4 + at, peers, stride=rows), :] = jnp.dot(
                pick, weight, preferred_element_type=F32, precision=HIGHEST
            )
    out_ref[pl.ds(8, peers, stride=rows), :] = wide
    out_ref[pl.ds(9, peers, stride=rows), :] = places


STATE_ROWS = 42


def state_pack(got_ref, x_ref, out_hbm, out_ref, sems):
    rows, stencil_rows = STATE_ROWS, STENCIL_ROWS
    peers = out_ref.shape[0] // rows
    total = x_ref.shape[1]
    new_rows = got_ref[pl.ds(8, peers, stride=stencil_rows), :].astype(I32)
    quarter = iota((1, LANES), 1) // 32
    tiles = []
    for tile in range(total // LANES):
        row = new_rows[4 * tile : 4 * tile + 1]
        for i in range(1, 4):
            row = jnp.where(quarter == i, new_rows[4 * tile + i : 4 * tile + i + 1], row)
        tiles.append(row)
    nid = jnp.concatenate(tiles, axis=1)
    high, low = split(x_ref[...])
    both = jnp.concatenate([high, low], axis=0).astype(BF16)
    lines = x_ref.shape[0]
    width = 2 * LANES
    own_cell = iota((8, LANES), 0) % 4 == iota((8, LANES), 1) // 32
    copies = []
    for chunk in range(total // width):
        pick = jnp.where(iota((width, total), 0) + chunk * width == nid, 1.0, 0.0).astype(BF16)
        moved = lax.dot_general(
            both, pick, (((1,), (1,)), ((), ())), preferred_element_type=F32
        )
        moved = moved[:lines] + moved[lines:]
        for tile in range(2):
            y = moved[:, tile * LANES : (tile + 1) * LANES]
            first = (chunk * 2 + tile) * 4
            for group in range(5):
                part = [y[(4 * group + i) * 8 : (4 * group + i + 1) * 8] for i in range(4)]
                turned = []
                for d in range(4):
                    diag = part[d]
                    for q in range(1, 4):
                        diag = jnp.where(quarter == q, part[(q + d) % 4], diag)
                    turned.append(diag if d == 0 else pltpu.roll(diag, 32 * d, 1))
                for q in range(4):
                    out = turned[(-q) % 4]
                    for i in range(1, 4):
                        out = jnp.where(quarter == i, turned[(i - q) % 4], out)
                    at = (first + q) * rows + 8 * group
                    out_ref[at : at + 8, :] = out
            rest = y[160:168]
            turned = [rest] + [pltpu.roll(rest, 32 * d, 1) for d in range(1, 4)]
            for q in range(4):
                out = turned[(-q) % 4]
                for i in range(1, 4):
                    out = jnp.where(quarter == i, turned[(i - q) % 4], out)
                out = jnp.where(own_cell, out, 0.0)
                at = (first + q) * rows + 40
                out_ref[at : at + 1, :] = jnp.sum(out[:4], axis=0, keepdims=True)
                out_ref[at + 1 : at + 2, :] = jnp.sum(out[4:], axis=0, keepdims=True)
        done = pl.ds(chunk * 8 * rows, 8 * rows)
        copy = pltpu.make_async_copy(out_ref.at[done, :], out_hbm.at[done, :], sems.at[chunk])
        copy.start()
        copies.append(copy)
    for copy in copies:
        copy.wait()


def stencil_place(
    got_ref, speed_ref, diffuse_ref, mixing_ref, low_ref, up_ref, wl_ref, wu_ref, lines_ref, mix_ref
):
    nv = mixing_ref.shape[0]
    high, low = split(0.25 * mixing_ref[...])
    by_row = (iota((mix_ref.shape[0], nv), 0) // 8 == iota((mix_ref.shape[0], nv), 1)).astype(F32)
    by_column = (iota((nv, 8 * nv), 0) == iota((nv, 8 * nv), 1) // 8).astype(F32)
    both = [
        jnp.dot(
            jnp.dot(by_row, part, preferred_element_type=F32),
            by_column,
            preferred_element_type=F32,
        )
        for part in (high, low)
    ]
    same = iota(both[0].shape, 0) % 8 == iota(both[0].shape, 1) % 8
    both = [jnp.where(same, part, 0.0) for part in both]
    rest = jnp.zeros((mix_ref.shape[0], mix_ref.shape[1] - 24 * nv), F32)
    mix_ref[...] = jnp.concatenate([both[0], both[0], both[1], rest], axis=1).astype(BF16)
    rows = STENCIL_ROWS
    peers = got_ref.shape[0] // rows
    stations = low_ref.shape[0] // 2
    spots = got_ref[pl.ds(9, peers, stride=rows), :].T
    place = iota((stations, peers), 0).astype(F32)
    picks = [jnp.where(spots[slot : slot + 1, :] == place, 1.0, 0.0) for slot in range(SLOTS)]
    for azim in range(2):
        idx = jnp.zeros((stations, LANES), F32)
        weight = jnp.zeros((stations, LANES), F32)
        for slot in range(SLOTS):
            at = rows_of(slot, azim)
            idx += jnp.dot(
                picks[slot],
                got_ref[pl.ds(at, peers, stride=rows), :],
                preferred_element_type=F32,
            )
            weight += jnp.dot(
                picks[slot],
                got_ref[pl.ds(4 + at, peers, stride=rows), :],
                preferred_element_type=F32,
                precision=HIGHEST,
            )
        live = idx >= 0.0
        low = jnp.where(live, idx, 0.0).astype(I32)
        up = low + 1
        here = pl.ds(azim * stations, stations)
        low_ref[here, :] = (low % 4) * 32 + low // 4
        up_ref[here, :] = (up % 4) * 32 + up // 4
        wl_ref[here, :] = jnp.where(live, 1.0 - weight, 0.0)
        wu_ref[here, :] = jnp.where(live, weight, 0.0)
        lines_ref[pl.ds(azim * stations, stations), :] = speed_ref[
            pl.ds(azim, stations, stride=2), :
        ]
        lines_ref[pl.ds((2 + azim) * stations, stations), :] = diffuse_ref[
            pl.ds(azim, stations, stride=2), :
        ]
        lines_ref[pl.ds((4 + azim) * stations, stations), :] = jnp.where(live, 1.0, 0.0)


def refit(got_ref, low_ref, up_ref, wl_ref, wu_ref, out_ref):
    rows = STATE_ROWS
    stations = low_ref.shape[0] // 2

    def lines(first_row):
        cells = [
            got_ref[pl.ds(block * 8 * rows + first_row + c, 8, stride=rows), :]
            for c in range(4)
            for block in range(4)
        ]
        return jnp.concatenate(cells, axis=0).T

    def fit(x, azim, line):
        here = pl.ds(azim * stations, stations)
        lower = jnp.take_along_axis(x, low_ref[here, :], axis=1)
        upper = jnp.take_along_axis(x, up_ref[here, :], axis=1)
        out_ref[pl.ds(line * stations, stations), :] = (
            wl_ref[here, :] * lower + wu_ref[here, :] * upper
        )

    for group in range(5):
        for half in range(2):
            x = lines(8 * group + 4 * half)
            for i in range(4):
                fit(x[i * stations : (i + 1) * stations], half, 8 * group + 2 * i + half)
    lane = iota((stations, LANES), 1)
    last = [got_ref[pl.ds(40 + half, stations, stride=rows), :] for half in range(2)]
    cells = []
    for c in range(4):
        a, b = [last[half] if c == half else pltpu.roll(last[half], (32 * (half - c)) % LANES, 1) for half in range(2)]
        cells.append(jnp.where(lane < 32, a, b))
    x = jnp.concatenate(cells, axis=0).T
    for half in range(2):
        fit(x[half * stations : (half + 1) * stations], half, 40 + half)


def mixed(mix, fields):
    nv = fields[0].shape[0]
    x = jnp.concatenate([f.reshape(nv * 8, LANES) for f in fields], axis=1)
    high, low = split(x)
    pad = jnp.zeros((mix.shape[1] - 24 * nv, x.shape[1]), F32)
    stacked = jnp.concatenate([high, low, high, pad], axis=0).astype(BF16)
    y = jnp.dot(mix, stacked, preferred_element_type=F32)[: nv * 8]
    return [y[:, i * LANES : (i + 1) * LANES].reshape(nv, 8, LANES) for i in range(len(fields))]


def line_of(ref, azim, block):
    return ref[:, pl.ds(azim * (ref.shape[1] // 2) + 8 * block, 8), :]


def coefficients(ref, azim, block):
    stations = ref.shape[0] // 6
    return [
        ref[pl.ds((2 * kind + azim) * stations + 8 * block, 8), :][None] for kind in range(3)
    ]


def slope(field):
    below = jnp.where(iota(field.shape, 2) == 0, 0.0, pltpu.roll(field, 1, 2))
    return field - below


def inner(m_ref, lines_ref, mix_ref, base_ref, term_ref):
    mix = mix_ref[...]
    stations = m_ref.shape[1] // 2
    for block in range(stations // 8):
        field = [line_of(m_ref, azim, block) for azim in range(2)]
        term = mixed(mix, field)
        base = []
        for azim in range(2):
            speed, diffuse, active = coefficients(lines_ref, azim, block)
            lateral = field[1 - azim] - 2.0 * field[azim]
            rate = diffuse * lateral - speed * slope(field[azim]) - term[azim]
            base.append(field[azim] + active * rate)
        term = mixed(mix, base)
        for azim in range(2):
            here = pl.ds(azim * stations + 8 * block, 8)
            base_ref[:, here, :] = base[azim]
            term_ref[:, here, :] = term[azim]


def sections(
    m_ref,
    base_ref,
    term_ref,
    left_ref,
    right_ref,
    lines_ref,
    lines_left_ref,
    lines_right_ref,
    mix_ref,
    out_hbm,
    out_ref,
    sems,
):
    mix = mix_ref[...]
    stations = m_ref.shape[1] // 2
    copies = []
    for block in range(stations // 8):
        field = [line_of(m_ref, azim, block) for azim in range(2)]
        near = [line_of(left_ref, 1, block), line_of(right_ref, 0, block)]
        far = [line_of(left_ref, 0, block), line_of(right_ref, 1, block)]
        outer = [
            coefficients(lines_left_ref, 1, block),
            coefficients(lines_right_ref, 0, block),
        ]
        own = [coefficients(lines_ref, azim, block) for azim in range(2)]
        near_term = mixed(mix, near)
        first = [
            line_of(base_ref, azim, block) + (own[azim][2] * own[azim][1]) * near[azim]
            for azim in range(2)
        ]
        for azim in range(2):
            speed, diffuse, active = outer[azim]
            lateral = (far[azim] + field[azim]) - 2.0 * near[azim]
            rate = diffuse * lateral - speed * slope(near[azim]) - near_term[azim]
            outside = near[azim] + active * rate
            speed, diffuse, active = own[azim]
            lateral = (outside + first[1 - azim]) - 2.0 * first[azim]
            term = line_of(term_ref, azim, block) + (active * diffuse) * near_term[azim]
            rate = diffuse * lateral - speed * slope(first[azim]) - term
            out = 0.5 * ((field[azim] + first[azim]) + active * rate)
            out_ref[:, pl.ds(azim + 16 * block, 8, stride=2), :] = out
        done = pl.ds(16 * block, 16)
        copy = pltpu.make_async_copy(
            out_ref.at[:, done, :], out_hbm.at[:, done, :], sems.at[block]
        )
        copy.start()
        copies.append(copy)
    for copy in copies:
        copy.wait()


def shards(
    state_in,
    new_index,
    stencil_index,
    stencil_weight,
    cell_count,
    normal_speed,
    azim_diffusion,
    mixing,
):
    peers = lax.axis_size("stream")
    count = lax.axis_size("azim")
    nv, total, _, cells = state_in.shape
    stations = new_index.shape[0]
    shape = jax.ShapeDtypeStruct

    def flat(a):
        return a.reshape(2 * stations, LANES)

    def exchange(a, rows, tile):
        parts = a.reshape(peers, rows // tile, tile, LANES)
        parts = lax.all_to_all(parts, "stream", split_axis=0, concat_axis=0, tiled=True)
        return parts.reshape(peers * rows, LANES)

    def neighbours(a):
        up = [(i, (i + 1) % count) for i in range(count)]
        down = [((i + 1) % count, i) for i in range(count)]
        return lax.ppermute(a, "azim", up), lax.ppermute(a, "azim", down)

    (packed,) = call(
        stencil_pack,
        [shape((peers * STENCIL_ROWS, LANES), F32)],
        new_index[None],
        flat(stencil_index),
        flat(stencil_weight),
        cell_count.T,
        space=pltpu.HBM,
        scratch=[
            pltpu.VMEM((1, stations), I32),
            pltpu.VMEM((2 * stations, LANES), I32),
            pltpu.VMEM((2 * stations, LANES), F32),
            pltpu.VMEM((2, stations), I32),
            pltpu.SemaphoreType.DMA((4,)),
        ],
        room=60,
    )
    got = exchange(packed, STENCIL_ROWS, 2)

    x = state_in.transpose(0, 2, 3, 1).reshape(nv * 2 * cells, total)
    (packed,) = call(
        state_pack,
        [shape((peers * STATE_ROWS, LANES), F32)],
        got,
        x,
        out_space=pltpu.HBM,
        scratch=[pltpu.VMEM((peers * STATE_ROWS, LANES), F32), pltpu.SemaphoreType.DMA((4,))],
    )
    got_state = exchange(packed, STATE_ROWS, 2)

    plane = shape((2 * stations, LANES), F32)
    index_plane = shape((2 * stations, LANES), I32)
    low, up, wl, wu, lines, mix = call(
        stencil_place,
        [
            index_plane,
            index_plane,
            plane,
            plane,
            shape((6 * stations, LANES), F32),
            shape((8 * nv + 8, 24 * nv + 8), BF16),
        ],
        got,
        flat(normal_speed),
        flat(azim_diffusion),
        mixing,
    )
    lines_left, lines_right = neighbours(lines)
    got_state, lines_left, lines_right = lax.optimization_barrier(
        (got_state, lines_left, lines_right)
    )

    (moved,) = call(
        refit, [shape((nv * 2 * stations, LANES), F32)], got_state, low, up, wl, wu
    )
    left, right = neighbours(moved)

    field = (nv, 2 * stations, LANES)
    moved = moved.reshape(field)
    base, term = call(inner, [shape(field, F32)] * 2, moved, lines, mix)
    (out,) = call(
        sections,
        [shape(field, F32)],
        moved,
        base,
        term,
        left.reshape(field),
        right.reshape(field),
        lines,
        lines_left,
        lines_right,
        mix,
        out_space=pltpu.HBM,
        scratch=[pltpu.VMEM(field, F32), pltpu.SemaphoreType.DMA((4,))],
    )
    return out.reshape(nv, stations, 2, LANES)


def solution(mesh):
    in_specs = (
        P(None, None, "azim", "stream"),
        P("stream"),
        P("stream", "azim", None),
        P("stream", "azim", None),
        P("stream", "azim"),
        P("stream", "azim", None),
        P("stream", "azim", None),
        P(),
    )
    out_specs = P(None, "stream", "azim", None)
    return jax.shard_map(shards, mesh=mesh, in_specs=in_specs, out_specs=out_specs, check_vma=False)
```

```python
import functools
import jax
import jax.numpy as jnp
from jax import lax
from jax.experimental import pallas as pl
from jax.experimental.pallas import tpu as pltpu
from jax.sharding import PartitionSpec as P

LANES = 128
SLOTS = 2
HIGHEST = lax.Precision.HIGHEST
F32 = jnp.float32
BF16 = jnp.bfloat16
I32 = jnp.int32


def call(body, outs, *args, space=pltpu.VMEM, out_space=pltpu.VMEM, scratch=(), room=24):
    touched = sum(a.size * a.dtype.itemsize for a in args) + sum(
        o.dtype.itemsize * functools.reduce(lambda x, y: x * y, o.shape) for o in outs
    )
    return pl.pallas_call(
        body,
        out_shape=outs,
        in_specs=[pl.BlockSpec(memory_space=space)] * len(args),
        out_specs=[pl.BlockSpec(memory_space=out_space)] * len(outs),
        scratch_shapes=list(scratch),
        compiler_params=pltpu.CompilerParams(vmem_limit_bytes=room * 2**20),
        cost_estimate=pl.CostEstimate(flops=0, bytes_accessed=touched, transcendentals=0),
    )(*args)


def iota(shape, dim):
    return lax.broadcasted_iota(I32, shape, dim)


def split(x):
    high = x.astype(BF16).astype(F32)
    return high, x - high


def rows_of(slot, azim):
    return slot * 2 + azim


STENCIL_ROWS = 10


def stencil_pack(nid_hbm, idx_hbm, weight_hbm, count_hbm, out_ref, nid_ref, idx_ref, weight_ref, count_ref, sems):
    pairs = [(nid_hbm, nid_ref), (count_hbm, count_ref), (idx_hbm, idx_ref), (weight_hbm, weight_ref)]
    copies = [pltpu.make_async_copy(a, b, sems.at[i]) for i, (a, b) in enumerate(pairs)]
    for copy in copies:
        copy.start()
    for copy in copies:
        copy.wait()
    rows = STENCIL_ROWS
    stations = idx_ref.shape[0] // 2
    peers = out_ref.shape[0] // rows
    nid = nid_ref[...]
    target = nid // stations
    place = nid % stations
    owners = (iota((peers, stations), 0) == target).astype(F32)
    before = (iota((stations, stations), 0) < iota((stations, stations), 1)).astype(F32)
    earlier = jnp.dot(owners, before, preferred_element_type=F32)
    rank = jnp.sum(owners * earlier, axis=0, keepdims=True)
    same = iota((stations, stations), 0) == iota((stations, stations), 1)
    spread = (iota((stations, LANES), 1) % stations == iota((stations, LANES), 0)).astype(F32)
    wide = jnp.dot(
        jnp.broadcast_to(nid.astype(F32), (peers, stations)),
        spread,
        preferred_element_type=F32,
        precision=HIGHEST,
    )
    lane = iota((peers, LANES), 1)
    places = jnp.full((peers, LANES), -1.0, F32)
    cell = iota((stations, LANES), 1)
    counts = [
        jnp.sum(jnp.where(same, count_ref[azim : azim + 1, :], 0), axis=1, keepdims=True)
        for azim in range(2)
    ]
    for slot in range(SLOTS):
        pick = jnp.where(rank == float(slot), owners, 0.0)
        found = jnp.sum(pick * (place + 1).astype(F32), axis=1, keepdims=True) - 1.0
        places = jnp.where(lane == slot, found, places)
        for azim in range(2):
            idx = idx_ref[pl.ds(azim, stations, stride=2), :]
            live = cell < counts[azim]
            idx = jnp.where(live, idx, -1).astype(F32)
            weight = weight_ref[pl.ds(azim, stations, stride=2), :]
            at = rows_of(slot, azim)
            out_ref[pl.ds(at, peers, stride=rows), :] = jnp.dot(
                pick, idx, preferred_element_type=F32
            )
            out_ref[pl.ds(4 + at, peers, stride=rows), :] = jnp.dot(
                pick, weight, preferred_element_type=F32, precision=HIGHEST
            )
    out_ref[pl.ds(8, peers, stride=rows), :] = wide
    out_ref[pl.ds(9, peers, stride=rows), :] = places


STATE_ROWS = 42


def state_pack(got_ref, x_ref, out_hbm, out_ref, sems):
    rows, stencil_rows = STATE_ROWS, STENCIL_ROWS
    peers = out_ref.shape[0] // rows
    total = x_ref.shape[1]
    new_rows = got_ref[pl.ds(8, peers, stride=stencil_rows), :].astype(I32)
    quarter = iota((1, LANES), 1) // 32
    tiles = []
    for tile in range(total // LANES):
        row = new_rows[4 * tile : 4 * tile + 1]
        for i in range(1, 4):
            row = jnp.where(quarter == i, new_rows[4 * tile + i : 4 * tile + i + 1], row)
        tiles.append(row)
    nid = jnp.concatenate(tiles, axis=1)
    high, low = split(x_ref[...])
    both = jnp.concatenate([high, low], axis=0).astype(BF16)
    lines = x_ref.shape[0]
    width = 2 * LANES
    own_cell = iota((8, LANES), 0) % 4 == iota((8, LANES), 1) // 32
    copies = []
    for chunk in range(total // width):
        pick = jnp.where(iota((width, total), 0) + chunk * width == nid, 1.0, 0.0).astype(BF16)
        moved = lax.dot_general(
            both, pick, (((1,), (1,)), ((), ())), preferred_element_type=F32
        )
        moved = moved[:lines] + moved[lines:]
        for tile in range(2):
            y = moved[:, tile * LANES : (tile + 1) * LANES]
            first = (chunk * 2 + tile) * 4
            for group in range(5):
                part = [y[(4 * group + i) * 8 : (4 * group + i + 1) * 8] for i in range(4)]
                turned = []
                for d in range(4):
                    diag = part[d]
                    for q in range(1, 4):
                        diag = jnp.where(quarter == q, part[(q + d) % 4], diag)
                    turned.append(diag if d == 0 else pltpu.roll(diag, 32 * d, 1))
                for q in range(4):
                    out = turned[(-q) % 4]
                    for i in range(1, 4):
                        out = jnp.where(quarter == i, turned[(i - q) % 4], out)
                    at = (first + q) * rows + 8 * group
                    out_ref[at : at + 8, :] = out
            rest = y[160:168]
            turned = [rest] + [pltpu.roll(rest, 32 * d, 1) for d in range(1, 4)]
            for q in range(4):
                out = turned[(-q) % 4]
                for i in range(1, 4):
                    out = jnp.where(quarter == i, turned[(i - q) % 4], out)
                out = jnp.where(own_cell, out, 0.0)
                at = (first + q) * rows + 40
                out_ref[at : at + 1, :] = jnp.sum(out[:4], axis=0, keepdims=True)
                out_ref[at + 1 : at + 2, :] = jnp.sum(out[4:], axis=0, keepdims=True)
        done = pl.ds(chunk * 8 * rows, 8 * rows)
        copy = pltpu.make_async_copy(out_ref.at[done, :], out_hbm.at[done, :], sems.at[chunk])
        copy.start()
        copies.append(copy)
    for copy in copies:
        copy.wait()


def stencil_place(
    got_ref, speed_ref, diffuse_ref, mixing_ref, low_ref, up_ref, wl_ref, wu_ref, lines_ref, mix_ref
):
    nv = mixing_ref.shape[0]
    high, low = split(0.25 * mixing_ref[...])
    by_row = (iota((mix_ref.shape[0], nv), 0) // 8 == iota((mix_ref.shape[0], nv), 1)).astype(F32)
    by_column = (iota((nv, 8 * nv), 0) == iota((nv, 8 * nv), 1) // 8).astype(F32)
    both = [
        jnp.dot(
            jnp.dot(by_row, part, preferred_element_type=F32),
            by_column,
            preferred_element_type=F32,
        )
        for part in (high, low)
    ]
    same = iota(both[0].shape, 0) % 8 == iota(both[0].shape, 1) % 8
    both = [jnp.where(same, part, 0.0) for part in both]
    rest = jnp.zeros((mix_ref.shape[0], mix_ref.shape[1] - 24 * nv), F32)
    mix_ref[...] = jnp.concatenate([both[0], both[0], both[1], rest], axis=1).astype(BF16)
    rows = STENCIL_ROWS
    peers = got_ref.shape[0] // rows
    stations = low_ref.shape[0] // 2
    spots = got_ref[pl.ds(9, peers, stride=rows), :].T
    place = iota((stations, peers), 0).astype(F32)
    picks = [jnp.where(spots[slot : slot + 1, :] == place, 1.0, 0.0) for slot in range(SLOTS)]
    for azim in range(2):
        idx = jnp.zeros((stations, LANES), F32)
        weight = jnp.zeros((stations, LANES), F32)
        for slot in range(SLOTS):
            at = rows_of(slot, azim)
            idx += jnp.dot(
                picks[slot],
                got_ref[pl.ds(at, peers, stride=rows), :],
                preferred_element_type=F32,
            )
            weight += jnp.dot(
                picks[slot],
                got_ref[pl.ds(4 + at, peers, stride=rows), :],
                preferred_element_type=F32,
                precision=HIGHEST,
            )
        live = idx >= 0.0
        low = jnp.where(live, idx, 0.0).astype(I32)
        up = low + 1
        here = pl.ds(azim * stations, stations)
        low_ref[here, :] = (low % 4) * 32 + low // 4
        up_ref[here, :] = (up % 4) * 32 + up // 4
        wl_ref[here, :] = jnp.where(live, 1.0 - weight, 0.0)
        wu_ref[here, :] = jnp.where(live, weight, 0.0)
        lines_ref[pl.ds(azim * stations, stations), :] = speed_ref[
            pl.ds(azim, stations, stride=2), :
        ]
        lines_ref[pl.ds((2 + azim) * stations, stations), :] = diffuse_ref[
            pl.ds(azim, stations, stride=2), :
        ]
        lines_ref[pl.ds((4 + azim) * stations, stations), :] = jnp.where(live, 1.0, 0.0)


def refit(got_ref, low_ref, up_ref, wl_ref, wu_ref, out_ref):
    rows = STATE_ROWS
    stations = low_ref.shape[0] // 2

    def lines(first_row):
        cells = [
            got_ref[pl.ds(block * 8 * rows + first_row + c, 8, stride=rows), :]
            for c in range(4)
            for block in range(4)
        ]
        return jnp.concatenate(cells, axis=0).T

    def fit(x, azim, line):
        here = pl.ds(azim * stations, stations)
        lower = jnp.take_along_axis(x, low_ref[here, :], axis=1)
        upper = jnp.take_along_axis(x, up_ref[here, :], axis=1)
        out_ref[pl.ds(line * stations, stations), :] = (
            wl_ref[here, :] * lower + wu_ref[here, :] * upper
        )

    for group in range(5):
        for half in range(2):
            x = lines(8 * group + 4 * half)
            for i in range(4):
                fit(x[i * stations : (i + 1) * stations], half, 8 * group + 2 * i + half)
    lane = iota((stations, LANES), 1)
    last = [got_ref[pl.ds(40 + half, stations, stride=rows), :] for half in range(2)]
    cells = []
    for c in range(4):
        a, b = [last[half] if c == half else pltpu.roll(last[half], (32 * (half - c)) % LANES, 1) for half in range(2)]
        cells.append(jnp.where(lane < 32, a, b))
    x = jnp.concatenate(cells, axis=0).T
    for half in range(2):
        fit(x[half * stations : (half + 1) * stations], half, 40 + half)


def mixed(mix, fields):
    nv = fields[0].shape[0]
    x = jnp.concatenate([f.reshape(nv * 8, LANES) for f in fields], axis=1)
    high, low = split(x)
    pad = jnp.zeros((mix.shape[1] - 24 * nv, x.shape[1]), F32)
    stacked = jnp.concatenate([high, low, high, pad], axis=0).astype(BF16)
    y = jnp.dot(mix, stacked, preferred_element_type=F32)[: nv * 8]
    return [y[:, i * LANES : (i + 1) * LANES].reshape(nv, 8, LANES) for i in range(len(fields))]


def line_of(ref, azim, block):
    return ref[:, pl.ds(azim * (ref.shape[1] // 2) + 8 * block, 8), :]


def coefficients(ref, azim, block):
    stations = ref.shape[0] // 6
    return [
        ref[pl.ds((2 * kind + azim) * stations + 8 * block, 8), :][None] for kind in range(3)
    ]


def slope(field):
    below = jnp.where(iota(field.shape, 2) == 0, 0.0, pltpu.roll(field, 1, 2))
    return field - below


def inner(m_ref, lines_ref, mix_ref, base_ref, term_ref):
    mix = mix_ref[...]
    stations = m_ref.shape[1] // 2
    for block in range(stations // 8):
        field = [line_of(m_ref, azim, block) for azim in range(2)]
        term = mixed(mix, field)
        base = []
        for azim in range(2):
            speed, diffuse, active = coefficients(lines_ref, azim, block)
            lateral = field[1 - azim] - 2.0 * field[azim]
            rate = diffuse * lateral - speed * slope(field[azim]) - term[azim]
            base.append(field[azim] + active * rate)
        term = mixed(mix, base)
        for azim in range(2):
            here = pl.ds(azim * stations + 8 * block, 8)
            base_ref[:, here, :] = base[azim]
            term_ref[:, here, :] = term[azim]


def sections(
    m_ref,
    base_ref,
    term_ref,
    right_ref,
    left_ref,
    lines_ref,
    lines_left_ref,
    lines_right_ref,
    mix_ref,
    out_hbm,
    out_ref,
    sems,
):
    mix = mix_ref[...]
    stations = m_ref.shape[1] // 2
    copies = []
    for block in range(stations // 8):
        field = [line_of(m_ref, azim, block) for azim in range(2)]
        near = [line_of(left_ref, 1, block), line_of(right_ref, 0, block)]
        far = [line_of(left_ref, 0, block), line_of(right_ref, 1, block)]
        outer = [
            coefficients(lines_left_ref, 1, block),
            coefficients(lines_right_ref, 0, block),
        ]
        own = [coefficients(lines_ref, azim, block) for azim in range(2)]
        near_term = mixed(mix, near)
        first = [
            line_of(base_ref, azim, block) + (own[azim][2] * own[azim][1]) * near[azim]
            for azim in range(2)
        ]
        for azim in range(2):
            speed, diffuse, active = outer[azim]
            lateral = (far[azim] + field[azim]) - 2.0 * near[azim]
            rate = diffuse * lateral - speed * slope(near[azim]) - near_term[azim]
            outside = near[azim] + active * rate
            speed, diffuse, active = own[azim]
            lateral = (outside + first[1 - azim]) - 2.0 * first[azim]
            term = line_of(term_ref, azim, block) + (active * diffuse) * near_term[azim]
            rate = diffuse * lateral - speed * slope(first[azim]) - term
            out = 0.5 * ((field[azim] + first[azim]) + active * rate)
            out_ref[:, pl.ds(azim + 16 * block, 8, stride=2), :] = out
        done = pl.ds(16 * block, 16)
        copy = pltpu.make_async_copy(
            out_ref.at[:, done, :], out_hbm.at[:, done, :], sems.at[block]
        )
        copy.start()
        copies.append(copy)
    for copy in copies:
        copy.wait()


def shards(
    state_in,
    new_index,
    stencil_index,
    stencil_weight,
    cell_count,
    normal_speed,
    azim_diffusion,
    mixing,
):
    peers = lax.axis_size("stream")
    count = lax.axis_size("azim")
    nv, total, _, cells = state_in.shape
    stations = new_index.shape[0]
    shape = jax.ShapeDtypeStruct

    def flat(a):
        return a.reshape(2 * stations, LANES)

    def exchange(a, rows, tile):
        parts = a.reshape(peers, rows // tile, tile, LANES)
        parts = lax.all_to_all(parts, "stream", split_axis=0, concat_axis=0, tiled=True)
        return parts.reshape(peers * rows, LANES)

    def neighbours(a):
        up = [(i, (i + 1) % count) for i in range(count)]
        down = [((i + 1) % count, i) for i in range(count)]
        return lax.ppermute(a, "azim", up), lax.ppermute(a, "azim", down)

    (packed,) = call(
        stencil_pack,
        [shape((peers * STENCIL_ROWS, LANES), F32)],
        new_index[None],
        flat(stencil_index),
        flat(stencil_weight),
        cell_count.T,
        space=pltpu.HBM,
        scratch=[
            pltpu.VMEM((1, stations), I32),
            pltpu.VMEM((2 * stations, LANES), I32),
            pltpu.VMEM((2 * stations, LANES), F32),
            pltpu.VMEM((2, stations), I32),
            pltpu.SemaphoreType.DMA((4,)),
        ],
        room=60,
    )
    got = exchange(packed, STENCIL_ROWS, 2)

    x = state_in.transpose(0, 2, 3, 1).reshape(nv * 2 * cells, total)
    (packed,) = call(
        state_pack,
        [shape((peers * STATE_ROWS, LANES), F32)],
        got,
        x,
        out_space=pltpu.HBM,
        scratch=[pltpu.VMEM((peers * STATE_ROWS, LANES), F32), pltpu.SemaphoreType.DMA((4,))],
    )
    got_state = exchange(packed, STATE_ROWS, 2)

    plane = shape((2 * stations, LANES), F32)
    index_plane = shape((2 * stations, LANES), I32)
    low, up, wl, wu, lines, mix = call(
        stencil_place,
        [
            index_plane,
            index_plane,
            plane,
            plane,
            shape((6 * stations, LANES), F32),
            shape((8 * nv + 8, 24 * nv + 8), BF16),
        ],
        got,
        flat(normal_speed),
        flat(azim_diffusion),
        mixing,
    )
    lines_left, lines_right = neighbours(lines)
    got_state, lines_left, lines_right = lax.optimization_barrier(
        (got_state, lines_left, lines_right)
    )

    (moved,) = call(
        refit, [shape((nv * 2 * stations, LANES), F32)], got_state, low, up, wl, wu
    )
    left, right = neighbours(moved)

    field = (nv, 2 * stations, LANES)
    moved = moved.reshape(field)
    base, term = call(inner, [shape(field, F32)] * 2, moved, lines, mix)
    (out,) = call(
        sections,
        [shape(field, F32)],
        moved,
        base,
        term,
        right.reshape(field),
        left.reshape(field),
        lines,
        lines_left,
        lines_right,
        mix,
        out_space=pltpu.HBM,
        scratch=[pltpu.VMEM(field, F32), pltpu.SemaphoreType.DMA((4,))],
    )
    return out.reshape(nv, stations, 2, LANES)


def solution(mesh):
    in_specs = (
        P(None, None, "azim", "stream"),
        P("stream"),
        P("stream", "azim", None),
        P("stream", "azim", None),
        P("stream", "azim"),
        P("stream", "azim", None),
        P("stream", "azim", None),
        P(),
    )
    out_specs = P(None, "stream", "azim", None)
    return jax.shard_map(shards, mesh=mesh, in_specs=in_specs, out_specs=out_specs, check_vma=False)
```

```python
import functools
import jax
import jax.numpy as jnp
from jax import lax
from jax.experimental import pallas as pl
from jax.experimental.pallas import tpu as pltpu
from jax.sharding import PartitionSpec as P

LANES = 128
SLOTS = 2
MARK = 1e30
HIGHEST = lax.Precision.HIGHEST
F32 = jnp.float32
BF16 = jnp.bfloat16
I32 = jnp.int32


def call(body, outs, *args, space=pltpu.VMEM, out_space=pltpu.VMEM, scratch=(), room=24):
    touched = sum(a.size * a.dtype.itemsize for a in args) + sum(
        o.dtype.itemsize * functools.reduce(lambda x, y: x * y, o.shape) for o in outs
    )
    return pl.pallas_call(
        body,
        out_shape=outs,
        in_specs=[pl.BlockSpec(memory_space=space)] * len(args),
        out_specs=[pl.BlockSpec(memory_space=out_space)] * len(outs),
        scratch_shapes=list(scratch),
        compiler_params=pltpu.CompilerParams(vmem_limit_bytes=room * 2**20),
        cost_estimate=pl.CostEstimate(flops=0, bytes_accessed=touched, transcendentals=0),
    )(*args)


def iota(shape, dim):
    return lax.broadcasted_iota(I32, shape, dim)


def split(x):
    high = x.astype(BF16).astype(F32)
    return high, x - high


def rows_of(slot, azim):
    return slot * 2 + azim


STENCIL_ROWS = 10


def stencil_pack(nid_hbm, idx_hbm, weight_hbm, count_hbm, out_ref, nid_ref, idx_ref, weight_ref, count_ref, sems):
    pairs = [(nid_hbm, nid_ref), (count_hbm, count_ref), (idx_hbm, idx_ref), (weight_hbm, weight_ref)]
    copies = [pltpu.make_async_copy(a, b, sems.at[i]) for i, (a, b) in enumerate(pairs)]
    for copy in copies:
        copy.start()
    for copy in copies:
        copy.wait()
    rows = STENCIL_ROWS
    stations = idx_ref.shape[0] // 2
    peers = out_ref.shape[0] // rows
    nid = nid_ref[...]
    target = nid // stations
    place = nid % stations
    owners = (iota((peers, stations), 0) == target).astype(F32)
    before = (iota((stations, stations), 0) < iota((stations, stations), 1)).astype(F32)
    earlier = jnp.dot(owners, before, preferred_element_type=F32)
    rank = jnp.sum(owners * earlier, axis=0, keepdims=True)
    same = iota((stations, stations), 0) == iota((stations, stations), 1)
    spread = (iota((stations, LANES), 1) % stations == iota((stations, LANES), 0)).astype(F32)
    wide = jnp.dot(
        jnp.broadcast_to(nid.astype(F32), (peers, stations)),
        spread,
        preferred_element_type=F32,
        precision=HIGHEST,
    )
    lane = iota((peers, LANES), 1)
    places = jnp.full((peers, LANES), -1.0, F32)
    cell = iota((stations, LANES), 1)
    counts = [
        jnp.sum(jnp.where(same, count_ref[azim : azim + 1, :], 0), axis=1, keepdims=True)
        for azim in range(2)
    ]
    for slot in range(SLOTS):
        pick = jnp.where(rank == float(slot), owners, 0.0)
        found = jnp.sum(pick * (place + 1).astype(F32), axis=1, keepdims=True) - 1.0
        places = jnp.where(lane == slot, found, places)
        for azim in range(2):
            idx = idx_ref[pl.ds(azim, stations, stride=2), :]
            live = cell < counts[azim]
            idx = jnp.where(live, idx, -1).astype(F32)
            weight = weight_ref[pl.ds(azim, stations, stride=2), :]
            at = rows_of(slot, azim)
            out_ref[pl.ds(at, peers, stride=rows), :] = jnp.dot(
                pick, idx, preferred_element_type=F32
            )
            out_ref[pl.ds(4 + at, peers, stride=rows), :] = jnp.dot(
                pick, weight, preferred_element_type=F32, precision=HIGHEST
            )
    out_ref[pl.ds(8, peers, stride=rows), :] = wide
    out_ref[pl.ds(9, peers, stride=rows), :] = places


def stencil_place(got_ref, low_ref, up_ref, wl_ref, wu_ref):
    rows = STENCIL_ROWS
    peers = got_ref.shape[0] // rows
    stations = low_ref.shape[0] // 2
    spots = got_ref[pl.ds(9, peers, stride=rows), :].T
    place = iota((stations, peers), 0).astype(F32)
    picks = [jnp.where(spots[slot : slot + 1, :] == place, 1.0, 0.0) for slot in range(SLOTS)]
    for azim in range(2):
        idx = jnp.zeros((stations, LANES), F32)
        weight = jnp.zeros((stations, LANES), F32)
        for slot in range(SLOTS):
            at = rows_of(slot, azim)
            idx += jnp.dot(
                picks[slot],
                got_ref[pl.ds(at, peers, stride=rows), :],
                preferred_element_type=F32,
            )
            weight += jnp.dot(
                picks[slot],
                got_ref[pl.ds(4 + at, peers, stride=rows), :],
                preferred_element_type=F32,
                precision=HIGHEST,
            )
        live = idx >= 0.0
        low = jnp.where(live, idx, 0.0).astype(I32)
        up = low + 1
        here = pl.ds(azim * stations, stations)
        low_ref[here, :] = (low % 4) * 32 + low // 4
        up_ref[here, :] = (up % 4) * 32 + up // 4
        wl_ref[here, :] = jnp.where(live, 1.0 - weight, 0.0)
        wu_ref[here, :] = jnp.where(live, weight, 0.0)


STATE_ROWS = 42


def state_pack(got_ref, x_ref, out_ref, low_ref, up_ref, wl_ref, wu_ref):
    rows, stencil_rows = STATE_ROWS, STENCIL_ROWS
    peers = out_ref.shape[0] // rows
    total = x_ref.shape[1]
    new_rows = got_ref[pl.ds(8, peers, stride=stencil_rows), :].astype(I32)
    quarter = iota((1, LANES), 1) // 32
    tiles = []
    for tile in range(total // LANES):
        row = new_rows[4 * tile : 4 * tile + 1]
        for i in range(1, 4):
            row = jnp.where(quarter == i, new_rows[4 * tile + i : 4 * tile + i + 1], row)
        tiles.append(row)
    nid = jnp.concatenate(tiles, axis=1)
    high, low = split(x_ref[...])
    both = jnp.concatenate([high, low], axis=0).astype(BF16)
    lines = x_ref.shape[0]
    width = 2 * LANES
    own_cell = iota((8, LANES), 0) % 4 == iota((8, LANES), 1) // 32
    for chunk in range(total // width):
        pick = jnp.where(iota((width, total), 0) + chunk * width == nid, 1.0, 0.0).astype(BF16)
        moved = lax.dot_general(
            both, pick, (((1,), (1,)), ((), ())), preferred_element_type=F32
        )
        moved = moved[:lines] + moved[lines:]
        for tile in range(2):
            y = moved[:, tile * LANES : (tile + 1) * LANES]
            first = (chunk * 2 + tile) * 4
            for group in range(5):
                part = [y[(4 * group + i) * 8 : (4 * group + i + 1) * 8] for i in range(4)]
                turned = []
                for d in range(4):
                    diag = part[d]
                    for q in range(1, 4):
                        diag = jnp.where(quarter == q, part[(q + d) % 4], diag)
                    turned.append(diag if d == 0 else pltpu.roll(diag, 32 * d, 1))
                for q in range(4):
                    out = turned[(-q) % 4]
                    for i in range(1, 4):
                        out = jnp.where(quarter == i, turned[(i - q) % 4], out)
                    at = (first + q) * rows + 8 * group
                    out_ref[at : at + 8, :] = out
            rest = y[160:168]
            turned = [rest] + [pltpu.roll(rest, 32 * d, 1) for d in range(1, 4)]
            for q in range(4):
                out = turned[(-q) % 4]
                for i in range(1, 4):
                    out = jnp.where(quarter == i, turned[(i - q) % 4], out)
                out = jnp.where(own_cell, out, 0.0)
                at = (first + q) * rows + 40
                out_ref[at : at + 1, :] = jnp.sum(out[:4], axis=0, keepdims=True)
                out_ref[at + 1 : at + 2, :] = jnp.sum(out[4:], axis=0, keepdims=True)
    stencil_place(got_ref, low_ref, up_ref, wl_ref, wu_ref)


def line_setup(speed_ref, diffuse_ref, mixing_ref, lines_ref, mix_ref):
    stations = speed_ref.shape[0] // 2
    for azim in range(2):
        here = pl.ds(azim, stations, stride=2)
        lines_ref[pl.ds(azim * stations, stations), :] = speed_ref[here, :]
        lines_ref[pl.ds((2 + azim) * stations, stations), :] = diffuse_ref[here, :]
    nv = mixing_ref.shape[0]
    high, low = split(0.25 * mixing_ref[...])
    by_row = (iota((mix_ref.shape[0], nv), 0) // 8 == iota((mix_ref.shape[0], nv), 1)).astype(F32)
    by_column = (iota((nv, 8 * nv), 0) == iota((nv, 8 * nv), 1) // 8).astype(F32)
    both = [
        jnp.dot(
            jnp.dot(by_row, part, preferred_element_type=F32),
            by_column,
            preferred_element_type=F32,
        )
        for part in (high, low)
    ]
    same = iota(both[0].shape, 0) % 8 == iota(both[0].shape, 1) % 8
    both = [jnp.where(same, part, 0.0) for part in both]
    rest = jnp.zeros((mix_ref.shape[0], mix_ref.shape[1] - 24 * nv), F32)
    mix_ref[...] = jnp.concatenate([both[0], both[0], both[1], rest], axis=1).astype(BF16)


def refit(got_ref, low_ref, up_ref, wl_ref, wu_ref, out_ref):
    rows = STATE_ROWS
    stations = low_ref.shape[0] // 2

    def lines(first_row):
        cells = [
            got_ref[pl.ds(block * 8 * rows + first_row + c, 8, stride=rows), :]
            for c in range(4)
            for block in range(4)
        ]
        return jnp.concatenate(cells, axis=0).T

    def fit(x, azim, line):
        here = pl.ds(azim * stations, stations)
        lower = jnp.take_along_axis(x, low_ref[here, :], axis=1)
        upper = jnp.take_along_axis(x, up_ref[here, :], axis=1)
        fitted = wl_ref[here, :] * lower + wu_ref[here, :] * upper
        if line < 2:
            fitted = jnp.where(wl_ref[here, :] + wu_ref[here, :] > 0.0, fitted, MARK)
        out_ref[pl.ds(line * stations, stations), :] = fitted

    for group in range(5):
        for half in range(2):
            x = lines(8 * group + 4 * half)
            for i in range(4):
                fit(x[i * stations : (i + 1) * stations], half, 8 * group + 2 * i + half)
    lane = iota((stations, LANES), 1)
    last = [got_ref[pl.ds(40 + half, stations, stride=rows), :] for half in range(2)]
    cells = []
    for c in range(4):
        a, b = [last[half] if c == half else pltpu.roll(last[half], (32 * (half - c)) % LANES, 1) for half in range(2)]
        cells.append(jnp.where(lane < 32, a, b))
    x = jnp.concatenate(cells, axis=0).T
    for half in range(2):
        fit(x[half * stations : (half + 1) * stations], half, 40 + half)


def mixed(mix, fields):
    nv = fields[0].shape[0]
    x = jnp.concatenate([f.reshape(nv * 8, LANES) for f in fields], axis=1)
    high, low = split(x)
    pad = jnp.zeros((mix.shape[1] - 24 * nv, x.shape[1]), F32)
    stacked = jnp.concatenate([high, low, high, pad], axis=0).astype(BF16)
    y = jnp.dot(mix, stacked, preferred_element_type=F32)[: nv * 8]
    return [y[:, i * LANES : (i + 1) * LANES].reshape(nv, 8, LANES) for i in range(len(fields))]


def line_of(ref, azim, block):
    return ref[:, pl.ds(azim * (ref.shape[1] // 2) + 8 * block, 8), :]


def marked_line(ref, azim, block):
    field = line_of(ref, azim, block)
    live = field[:1] < 0.5 * MARK
    first = jnp.where(live, field[:1], 0.0)
    return jnp.concatenate([first, field[1:]], axis=0), jnp.where(live, 1.0, 0.0)


def coefficients(ref, azim, block):
    stations = ref.shape[0] // 4
    return [
        ref[pl.ds((2 * kind + azim) * stations + 8 * block, 8), :][None] for kind in range(2)
    ]


def slope(field):
    below = jnp.where(iota(field.shape, 2) == 0, 0.0, pltpu.roll(field, 1, 2))
    return field - below


def inner(m_ref, lines_ref, mix_ref, base_ref, term_ref):
    mix = mix_ref[...]
    stations = m_ref.shape[1] // 2
    for block in range(stations // 8):
        field, live = zip(*[marked_line(m_ref, azim, block) for azim in range(2)])
        term = mixed(mix, field)
        base = []
        for azim in range(2):
            speed, diffuse = coefficients(lines_ref, azim, block)
            active = live[azim]
            lateral = field[1 - azim] - 2.0 * field[azim]
            rate = diffuse * lateral - speed * slope(field[azim]) - term[azim]
            base.append(field[azim] + active * rate)
        term = mixed(mix, base)
        for azim in range(2):
            here = pl.ds(azim * stations + 8 * block, 8)
            base_ref[:, here, :] = base[azim]
            term_ref[:, here, :] = term[azim]


def sections(
    m_ref,
    base_ref,
    term_ref,
    right_ref,
    left_ref,
    lines_ref,
    lines_left_ref,
    lines_right_ref,
    mix_ref,
    out_hbm,
    out_ref,
    sems,
):
    mix = mix_ref[...]
    stations = m_ref.shape[1] // 2
    copies = []
    for block in range(stations // 8):
        field, live = zip(*[marked_line(m_ref, azim, block) for azim in range(2)])
        near, near_live = zip(
            marked_line(left_ref, 1, block), marked_line(right_ref, 0, block)
        )
        far = [marked_line(left_ref, 0, block)[0], marked_line(right_ref, 1, block)[0]]
        outer = [
            coefficients(lines_left_ref, 1, block),
            coefficients(lines_right_ref, 0, block),
        ]
        own = [coefficients(lines_ref, azim, block) for azim in range(2)]
        near_term = mixed(mix, near)
        first = [
            line_of(base_ref, azim, block) + (live[azim] * own[azim][1]) * near[azim]
            for azim in range(2)
        ]
        for azim in range(2):
            speed, diffuse = outer[azim]
            lateral = (far[azim] + field[azim]) - 2.0 * near[azim]
            rate = diffuse * lateral - speed * slope(near[azim]) - near_term[azim]
            outside = near[azim] + near_live[azim] * rate
            speed, diffuse = own[azim]
            active = live[azim]
            lateral = (outside + first[1 - azim]) - 2.0 * first[azim]
            term = line_of(term_ref, azim, block) + (active * diffuse) * near_term[azim]
            rate = diffuse * lateral - speed * slope(first[azim]) - term
            out = 0.5 * ((field[azim] + first[azim]) + active * rate)
            out_ref[:, pl.ds(azim + 16 * block, 8, stride=2), :] = out
        done = pl.ds(16 * block, 16)
        copy = pltpu.make_async_copy(
            out_ref.at[:, done, :], out_hbm.at[:, done, :], sems.at[block]
        )
        copy.start()
        copies.append(copy)
    for copy in copies:
        copy.wait()


def shards(
    state_in,
    new_index,
    stencil_index,
    stencil_weight,
    cell_count,
    normal_speed,
    azim_diffusion,
    mixing,
):
    peers = lax.axis_size("stream")
    count = lax.axis_size("azim")
    nv, total, _, cells = state_in.shape
    stations = new_index.shape[0]
    shape = jax.ShapeDtypeStruct

    def flat(a):
        return a.reshape(2 * stations, LANES)

    def exchange(a, rows, tile):
        parts = a.reshape(peers, rows // tile, tile, LANES)
        parts = lax.all_to_all(parts, "stream", split_axis=0, concat_axis=0, tiled=True)
        return parts.reshape(peers * rows, LANES)

    def neighbours(a):
        up = [(i, (i + 1) % count) for i in range(count)]
        down = [((i + 1) % count, i) for i in range(count)]
        return lax.ppermute(a, "azim", up), lax.ppermute(a, "azim", down)

    (packed,) = call(
        stencil_pack,
        [shape((peers * STENCIL_ROWS, LANES), F32)],
        new_index[None],
        flat(stencil_index),
        flat(stencil_weight),
        cell_count.T,
        space=pltpu.HBM,
        scratch=[
            pltpu.VMEM((1, stations), I32),
            pltpu.VMEM((2 * stations, LANES), I32),
            pltpu.VMEM((2 * stations, LANES), F32),
            pltpu.VMEM((2, stations), I32),
            pltpu.SemaphoreType.DMA((4,)),
        ],
        room=60,
    )
    got = exchange(packed, STENCIL_ROWS, 2)

    lines, mix = call(
        line_setup,
        [shape((4 * stations, LANES), F32), shape((8 * nv + 8, 24 * nv + 8), BF16)],
        flat(normal_speed),
        flat(azim_diffusion),
        mixing,
    )
    lines_left, lines_right = neighbours(lines)

    x = state_in.transpose(0, 2, 3, 1).reshape(nv * 2 * cells, total)
    plane = shape((2 * stations, LANES), F32)
    index_plane = shape((2 * stations, LANES), I32)
    packed, low, up, wl, wu = call(
        state_pack,
        [shape((peers * STATE_ROWS, LANES), F32), index_plane, index_plane, plane, plane],
        got,
        x,
    )
    packed, lines_left, lines_right, mix = lax.optimization_barrier(
        (packed, lines_left, lines_right, mix)
    )
    got_state = exchange(packed, STATE_ROWS, 2)

    (moved,) = call(
        refit, [shape((nv * 2 * stations, LANES), F32)], got_state, low, up, wl, wu
    )
    left, right = neighbours(moved)

    field = (nv, 2 * stations, LANES)
    moved = moved.reshape(field)
    base, term = call(inner, [shape(field, F32)] * 2, moved, lines, mix)
    (out,) = call(
        sections,
        [shape(field, F32)],
        moved,
        base,
        term,
        right.reshape(field),
        left.reshape(field),
        lines,
        lines_left,
        lines_right,
        mix,
        out_space=pltpu.HBM,
        scratch=[pltpu.VMEM(field, F32), pltpu.SemaphoreType.DMA((4,))],
    )
    return out.reshape(nv, stations, 2, LANES)


def solution(mesh):
    in_specs = (
        P(None, None, "azim", "stream"),
        P("stream"),
        P("stream", "azim", None),
        P("stream", "azim", None),
        P("stream", "azim"),
        P("stream", "azim", None),
        P("stream", "azim", None),
        P(),
    )
    out_specs = P(None, "stream", "azim", None)
    return jax.shard_map(shards, mesh=mesh, in_specs=in_specs, out_specs=out_specs, check_vma=False)
```

```python
import functools
import jax
import jax.numpy as jnp
from jax import lax
from jax.experimental import pallas as pl
from jax.experimental.pallas import tpu as pltpu
from jax.sharding import PartitionSpec as P

LANES = 128
SLOTS = 2
MARK = 1e30
HIGHEST = lax.Precision.HIGHEST
F32 = jnp.float32
BF16 = jnp.bfloat16
I32 = jnp.int32


def call(body, outs, *args, space=pltpu.VMEM, out_space=pltpu.VMEM, scratch=(), room=24):
    touched = sum(a.size * a.dtype.itemsize for a in args) + sum(
        o.dtype.itemsize * functools.reduce(lambda x, y: x * y, o.shape) for o in outs
    )
    return pl.pallas_call(
        body,
        out_shape=outs,
        in_specs=[pl.BlockSpec(memory_space=space)] * len(args),
        out_specs=[pl.BlockSpec(memory_space=out_space)] * len(outs),
        scratch_shapes=list(scratch),
        compiler_params=pltpu.CompilerParams(vmem_limit_bytes=room * 2**20),
        cost_estimate=pl.CostEstimate(flops=0, bytes_accessed=touched, transcendentals=0),
    )(*args)


def iota(shape, dim):
    return lax.broadcasted_iota(I32, shape, dim)


def split(x):
    high = x.astype(BF16).astype(F32)
    return high, x - high


def rows_of(slot, azim):
    return slot * 2 + azim


STENCIL_ROWS = 10


def stencil_pack(nid_hbm, idx_hbm, weight_hbm, count_hbm, out_ref, nid_ref, idx_ref, weight_ref, count_ref, sems):
    pairs = [(nid_hbm, nid_ref), (count_hbm, count_ref), (idx_hbm, idx_ref), (weight_hbm, weight_ref)]
    copies = [pltpu.make_async_copy(a, b, sems.at[i]) for i, (a, b) in enumerate(pairs)]
    for copy in copies:
        copy.start()
    for copy in copies:
        copy.wait()
    rows = STENCIL_ROWS
    stations = idx_ref.shape[0] // 2
    peers = out_ref.shape[0] // rows
    nid = nid_ref[...]
    target = nid // stations
    place = nid % stations
    owners = (iota((peers, stations), 0) == target).astype(F32)
    before = (iota((stations, stations), 0) < iota((stations, stations), 1)).astype(F32)
    earlier = jnp.dot(owners, before, preferred_element_type=F32)
    rank = jnp.sum(owners * earlier, axis=0, keepdims=True)
    same = iota((stations, stations), 0) == iota((stations, stations), 1)
    spread = (iota((stations, LANES), 1) % stations == iota((stations, LANES), 0)).astype(F32)
    wide = jnp.dot(
        jnp.broadcast_to(nid.astype(F32), (peers, stations)),
        spread,
        preferred_element_type=F32,
        precision=HIGHEST,
    )
    lane = iota((peers, LANES), 1)
    places = jnp.full((peers, LANES), -1.0, F32)
    cell = iota((stations, LANES), 1)
    counts = [
        jnp.sum(jnp.where(same, count_ref[azim : azim + 1, :], 0), axis=1, keepdims=True)
        for azim in range(2)
    ]
    for slot in range(SLOTS):
        pick = jnp.where(rank == float(slot), owners, 0.0)
        found = jnp.sum(pick * (place + 1).astype(F32), axis=1, keepdims=True) - 1.0
        places = jnp.where(lane == slot, found, places)
        for azim in range(2):
            idx = idx_ref[pl.ds(azim, stations, stride=2), :]
            live = cell < counts[azim]
            idx = jnp.where(live, idx, -1).astype(F32)
            weight = weight_ref[pl.ds(azim, stations, stride=2), :]
            at = rows_of(slot, azim)
            out_ref[pl.ds(at, peers, stride=rows), :] = jnp.dot(
                pick, idx, preferred_element_type=F32
            )
            out_ref[pl.ds(4 + at, peers, stride=rows), :] = jnp.dot(
                pick, weight, preferred_element_type=F32, precision=HIGHEST
            )
    out_ref[pl.ds(8, peers, stride=rows), :] = wide
    out_ref[pl.ds(9, peers, stride=rows), :] = places


def stencil_place(got_ref, low_ref, up_ref, wl_ref, wu_ref):
    rows = STENCIL_ROWS
    peers = got_ref.shape[0] // rows
    stations = low_ref.shape[0] // 2
    spots = got_ref[pl.ds(9, peers, stride=rows), :].T
    place = iota((stations, peers), 0).astype(F32)
    picks = [jnp.where(spots[slot : slot + 1, :] == place, 1.0, 0.0) for slot in range(SLOTS)]
    for azim in range(2):
        idx = jnp.zeros((stations, LANES), F32)
        weight = jnp.zeros((stations, LANES), F32)
        for slot in range(SLOTS):
            at = rows_of(slot, azim)
            idx += jnp.dot(
                picks[slot],
                got_ref[pl.ds(at, peers, stride=rows), :],
                preferred_element_type=F32,
            )
            weight += jnp.dot(
                picks[slot],
                got_ref[pl.ds(4 + at, peers, stride=rows), :],
                preferred_element_type=F32,
                precision=HIGHEST,
            )
        live = idx >= 0.0
        low = jnp.where(live, idx, 0.0).astype(I32)
        up = low + 1
        here = pl.ds(azim * stations, stations)
        low_ref[here, :] = (low % 4) * 32 + low // 4
        up_ref[here, :] = (up % 4) * 32 + up // 4
        wl_ref[here, :] = jnp.where(live, 1.0 - weight, 0.0)
        wu_ref[here, :] = jnp.where(live, weight, 0.0)


STATE_ROWS = 42


def state_pack(got_ref, x_ref, out_ref, low_ref, up_ref, wl_ref, wu_ref):
    rows, stencil_rows = STATE_ROWS, STENCIL_ROWS
    peers = out_ref.shape[0] // rows
    total = x_ref.shape[1]
    new_rows = got_ref[pl.ds(8, peers, stride=stencil_rows), :].astype(I32)
    quarter = iota((1, LANES), 1) // 32
    tiles = []
    for tile in range(total // LANES):
        row = new_rows[4 * tile : 4 * tile + 1]
        for i in range(1, 4):
            row = jnp.where(quarter == i, new_rows[4 * tile + i : 4 * tile + i + 1], row)
        tiles.append(row)
    nid = jnp.concatenate(tiles, axis=1)
    stations = total // peers
    owner = jnp.broadcast_to((nid // stations).astype(F32), (16, total)).astype(BF16)
    place = jnp.where(iota((stations, total), 0) == nid % stations, 1.0, 0.0).astype(BF16)
    none = jnp.zeros((16, total), BF16)
    high, low = split(x_ref[...])
    both = jnp.concatenate([high, low], axis=0).astype(BF16)
    lines = x_ref.shape[0]
    width = 2 * LANES
    own_cell = iota((8, LANES), 0) % 4 == iota((8, LANES), 1) // 32
    for chunk in range(total // width):
        rows_here = []
        for peer in range(chunk * 8, chunk * 8 + 8):
            mine = owner == jnp.bfloat16(peer)
            rows_here += [
                jnp.where(mine, place[at : at + 16], none) for at in range(0, stations, 16)
            ]
        pick = jnp.concatenate(rows_here, axis=0)
        moved = lax.dot_general(
            both, pick, (((1,), (1,)), ((), ())), preferred_element_type=F32
        )
        moved = moved[:lines] + moved[lines:]
        for tile in range(2):
            y = moved[:, tile * LANES : (tile + 1) * LANES]
            first = (chunk * 2 + tile) * 4
            for group in range(5):
                part = [y[(4 * group + i) * 8 : (4 * group + i + 1) * 8] for i in range(4)]
                turned = []
                for d in range(4):
                    diag = part[d]
                    for q in range(1, 4):
                        diag = jnp.where(quarter == q, part[(q + d) % 4], diag)
                    turned.append(diag if d == 0 else pltpu.roll(diag, 32 * d, 1))
                for q in range(4):
                    out = turned[(-q) % 4]
                    for i in range(1, 4):
                        out = jnp.where(quarter == i, turned[(i - q) % 4], out)
                    at = (first + q) * rows + 8 * group
                    out_ref[at : at + 8, :] = out
            rest = y[160:168]
            turned = [rest] + [pltpu.roll(rest, 32 * d, 1) for d in range(1, 4)]
            for q in range(4):
                out = turned[(-q) % 4]
                for i in range(1, 4):
                    out = jnp.where(quarter == i, turned[(i - q) % 4], out)
                out = jnp.where(own_cell, out, 0.0)
                at = (first + q) * rows + 40
                out_ref[at : at + 1, :] = jnp.sum(out[:4], axis=0, keepdims=True)
                out_ref[at + 1 : at + 2, :] = jnp.sum(out[4:], axis=0, keepdims=True)
    stencil_place(got_ref, low_ref, up_ref, wl_ref, wu_ref)


def line_setup(speed_ref, diffuse_ref, mixing_ref, lines_ref, mix_ref):
    stations = speed_ref.shape[0] // 2
    for azim in range(2):
        here = pl.ds(azim, stations, stride=2)
        lines_ref[pl.ds(azim * stations, stations), :] = speed_ref[here, :]
        lines_ref[pl.ds((2 + azim) * stations, stations), :] = diffuse_ref[here, :]
    nv = mixing_ref.shape[0]
    high, low = split(0.25 * mixing_ref[...])
    by_row = (iota((mix_ref.shape[0], nv), 0) // 8 == iota((mix_ref.shape[0], nv), 1)).astype(F32)
    by_column = (iota((nv, 8 * nv), 0) == iota((nv, 8 * nv), 1) // 8).astype(F32)
    both = [
        jnp.dot(
            jnp.dot(by_row, part, preferred_element_type=F32),
            by_column,
            preferred_element_type=F32,
        )
        for part in (high, low)
    ]
    same = iota(both[0].shape, 0) % 8 == iota(both[0].shape, 1) % 8
    both = [jnp.where(same, part, 0.0) for part in both]
    rest = jnp.zeros((mix_ref.shape[0], mix_ref.shape[1] - 24 * nv), F32)
    mix_ref[...] = jnp.concatenate([both[0], both[0], both[1], rest], axis=1).astype(BF16)


def refit(got_ref, low_ref, up_ref, wl_ref, wu_ref, out_ref):
    rows = STATE_ROWS
    stations = low_ref.shape[0] // 2

    def lines(first_row):
        cells = [
            got_ref[pl.ds(block * 8 * rows + first_row + c, 8, stride=rows), :]
            for c in range(4)
            for block in range(4)
        ]
        return jnp.concatenate(cells, axis=0).T

    def read(ref):
        return [ref[pl.ds(azim * stations, stations), :] for azim in range(2)]

    low, up, wl, wu = read(low_ref), read(up_ref), read(wl_ref), read(wu_ref)

    def take(x, index):
        return jnp.take_along_axis(x, index, axis=1, mode="promise_in_bounds")

    def fit(x, azim, line):
        fitted = wl[azim] * take(x, low[azim]) + wu[azim] * take(x, up[azim])
        if line < 2:
            fitted = jnp.where(wl[azim] + wu[azim] > 0.0, fitted, MARK)
        out_ref[pl.ds(line * stations, stations), :] = fitted

    for group in range(5):
        for half in range(2):
            x = lines(8 * group + 4 * half)
            for i in range(4):
                fit(x[i * stations : (i + 1) * stations], half, 8 * group + 2 * i + half)
    lane = iota((stations, LANES), 1)
    last = [got_ref[pl.ds(40 + half, stations, stride=rows), :] for half in range(2)]
    cells = []
    for c in range(4):
        a, b = [last[half] if c == half else pltpu.roll(last[half], (32 * (half - c)) % LANES, 1) for half in range(2)]
        cells.append(jnp.where(lane < 32, a, b))
    x = jnp.concatenate(cells, axis=0).T
    for half in range(2):
        fit(x[half * stations : (half + 1) * stations], half, 40 + half)


def mixed(mix, fields):
    nv = fields[0].shape[0]
    x = jnp.concatenate([f.reshape(nv * 8, LANES) for f in fields], axis=1)
    high, low = split(x)
    pad = jnp.zeros((mix.shape[1] - 24 * nv, x.shape[1]), F32)
    stacked = jnp.concatenate([high, low, high, pad], axis=0).astype(BF16)
    y = jnp.dot(mix, stacked, preferred_element_type=F32)[: nv * 8]
    return [y[:, i * LANES : (i + 1) * LANES].reshape(nv, 8, LANES) for i in range(len(fields))]


def line_of(ref, azim, block):
    return ref[:, pl.ds(azim * (ref.shape[1] // 2) + 8 * block, 8), :]


def marked_line(ref, azim, block):
    field = line_of(ref, azim, block)
    live = field[:1] < 0.5 * MARK
    first = jnp.where(live, field[:1], 0.0)
    return jnp.concatenate([first, field[1:]], axis=0), jnp.where(live, 1.0, 0.0)


def coefficients(ref, azim, block):
    stations = ref.shape[0] // 4
    return [
        ref[pl.ds((2 * kind + azim) * stations + 8 * block, 8), :][None] for kind in range(2)
    ]


def factors(ref, azim, block, active):
    speed, diffuse = coefficients(ref, azim, block)
    side, below = active * diffuse, active * speed
    own = 1.0 - (2.0 * side + below)
    return own, side, jnp.where(iota(below.shape, 2) == 0, 0.0, below)


def shifted(field):
    return pltpu.roll(field, 1, 2)


def inner(m_ref, lines_ref, mix_ref, base_ref, rest_ref):
    mix = mix_ref[...]
    stations = m_ref.shape[1] // 2
    for block in range(stations // 8):
        field, live = zip(*[marked_line(m_ref, azim, block) for azim in range(2)])
        term = mixed(mix, field)
        base = []
        for azim in range(2):
            own, side, below = factors(lines_ref, azim, block, live[azim])
            base.append(
                (own * field[azim] + side * field[1 - azim])
                + (below * shifted(field[azim]) - live[azim] * term[azim])
            )
        term = mixed(mix, base)
        for azim in range(2):
            here = pl.ds(azim * stations + 8 * block, 8)
            base_ref[:, here, :] = base[azim]
            rest_ref[:, here, :] = 0.5 * (field[azim] - live[azim] * term[azim])


def sections(
    m_ref,
    base_ref,
    rest_ref,
    right_ref,
    left_ref,
    lines_ref,
    lines_left_ref,
    lines_right_ref,
    mix_ref,
    out_hbm,
    out_ref,
    sems,
):
    mix = mix_ref[...]
    stations = m_ref.shape[1] // 2
    copies = []
    for block in range(stations // 8):
        field, live = zip(*[marked_line(m_ref, azim, block) for azim in range(2)])
        near, near_live = zip(
            marked_line(left_ref, 1, block), marked_line(right_ref, 0, block)
        )
        far = [marked_line(left_ref, 0, block)[0], marked_line(right_ref, 1, block)[0]]
        outer = [
            factors(lines_left_ref, 1, block, near_live[0]),
            factors(lines_right_ref, 0, block, near_live[1]),
        ]
        inside = [factors(lines_ref, azim, block, live[azim]) for azim in range(2)]
        near_term = mixed(mix, near)
        first = [
            line_of(base_ref, azim, block) + inside[azim][1] * near[azim] for azim in range(2)
        ]
        for azim in range(2):
            own, side, below = outer[azim]
            beyond = (own * near[azim] + side * (far[azim] + field[azim])) + (
                below * shifted(near[azim]) - near_live[azim] * near_term[azim]
            )
            own, side, below = [0.5 * factor for factor in inside[azim]]
            out = (
                (line_of(rest_ref, azim, block) + own * first[azim])
                + side * ((beyond + first[1 - azim]) - near_term[azim])
                + below * shifted(first[azim])
            )
            out_ref[:, pl.ds(azim + 16 * block, 8, stride=2), :] = out
        done = pl.ds(16 * block, 16)
        copy = pltpu.make_async_copy(
            out_ref.at[:, done, :], out_hbm.at[:, done, :], sems.at[block]
        )
        copy.start()
        copies.append(copy)
    for copy in copies:
        copy.wait()


def shards(
    state_in,
    new_index,
    stencil_index,
    stencil_weight,
    cell_count,
    normal_speed,
    azim_diffusion,
    mixing,
):
    peers = lax.axis_size("stream")
    count = lax.axis_size("azim")
    nv, total, _, cells = state_in.shape
    stations = new_index.shape[0]
    shape = jax.ShapeDtypeStruct

    def flat(a):
        return a.reshape(2 * stations, LANES)

    def exchange(a, rows, tile):
        parts = a.reshape(peers, rows // tile, tile, LANES)
        parts = lax.all_to_all(parts, "stream", split_axis=0, concat_axis=0, tiled=True)
        return parts.reshape(peers * rows, LANES)

    def neighbours(a):
        up = [(i, (i + 1) % count) for i in range(count)]
        down = [((i + 1) % count, i) for i in range(count)]
        return lax.ppermute(a, "azim", up), lax.ppermute(a, "azim", down)

    (packed,) = call(
        stencil_pack,
        [shape((peers * STENCIL_ROWS, LANES), F32)],
        new_index[None],
        flat(stencil_index),
        flat(stencil_weight),
        cell_count.T,
        space=pltpu.HBM,
        scratch=[
            pltpu.VMEM((1, stations), I32),
            pltpu.VMEM((2 * stations, LANES), I32),
            pltpu.VMEM((2 * stations, LANES), F32),
            pltpu.VMEM((2, stations), I32),
            pltpu.SemaphoreType.DMA((4,)),
        ],
        room=60,
    )
    got = exchange(packed, STENCIL_ROWS, 2)

    lines, mix = call(
        line_setup,
        [shape((4 * stations, LANES), F32), shape((8 * nv + 8, 24 * nv + 8), BF16)],
        flat(normal_speed),
        flat(azim_diffusion),
        mixing,
    )
    lines_left, lines_right = neighbours(lines)

    x = state_in.transpose(0, 2, 3, 1).reshape(nv * 2 * cells, total)
    plane = shape((2 * stations, LANES), F32)
    index_plane = shape((2 * stations, LANES), I32)
    packed, low, up, wl, wu = call(
        state_pack,
        [shape((peers * STATE_ROWS, LANES), F32), index_plane, index_plane, plane, plane],
        got,
        x,
    )
    packed, lines_left, lines_right, mix = lax.optimization_barrier(
        (packed, lines_left, lines_right, mix)
    )
    got_state = exchange(packed, STATE_ROWS, 2)

    (moved,) = call(
        refit, [shape((nv * 2 * stations, LANES), F32)], got_state, low, up, wl, wu
    )
    left, right = neighbours(moved)

    field = (nv, 2 * stations, LANES)
    moved = moved.reshape(field)
    base, rest = call(inner, [shape(field, F32)] * 2, moved, lines, mix)
    (out,) = call(
        sections,
        [shape(field, F32)],
        moved,
        base,
        rest,
        right.reshape(field),
        left.reshape(field),
        lines,
        lines_left,
        lines_right,
        mix,
        out_space=pltpu.HBM,
        scratch=[pltpu.VMEM(field, F32), pltpu.SemaphoreType.DMA((4,))],
    )
    return out.reshape(nv, stations, 2, LANES)


def solution(mesh):
    in_specs = (
        P(None, None, "azim", "stream"),
        P("stream"),
        P("stream", "azim", None),
        P("stream", "azim", None),
        P("stream", "azim"),
        P("stream", "azim", None),
        P("stream", "azim", None),
        P(),
    )
    out_specs = P(None, "stream", "azim", None)
    return jax.shard_map(shards, mesh=mesh, in_specs=in_specs, out_specs=out_specs, check_vma=False)
```

```python
import functools
import jax
import jax.numpy as jnp
from jax import lax
from jax.experimental import pallas as pl
from jax.experimental.pallas import tpu as pltpu
from jax.sharding import PartitionSpec as P

LANES = 128
SLOTS = 2
MARK = 1e30
HIGHEST = lax.Precision.HIGHEST
F32 = jnp.float32
BF16 = jnp.bfloat16
I32 = jnp.int32


def call(body, outs, *args, space=pltpu.VMEM, out_space=pltpu.VMEM, scratch=(), room=24):
    touched = sum(a.size * a.dtype.itemsize for a in args) + sum(
        o.dtype.itemsize * functools.reduce(lambda x, y: x * y, o.shape) for o in outs
    )
    return pl.pallas_call(
        body,
        out_shape=outs,
        in_specs=[pl.BlockSpec(memory_space=space)] * len(args),
        out_specs=[pl.BlockSpec(memory_space=out_space)] * len(outs),
        scratch_shapes=list(scratch),
        compiler_params=pltpu.CompilerParams(vmem_limit_bytes=room * 2**20),
        cost_estimate=pl.CostEstimate(flops=0, bytes_accessed=touched, transcendentals=0),
    )(*args)


def iota(shape, dim):
    return lax.broadcasted_iota(I32, shape, dim)


def split(x):
    high = x.astype(BF16).astype(F32)
    return high, x - high


def rows_of(slot, azim):
    return slot * 2 + azim


STENCIL_ROWS = 10


def stencil_pack(nid_hbm, idx_hbm, weight_hbm, count_hbm, out_ref, nid_ref, idx_ref, weight_ref, count_ref, sems):
    pairs = [(nid_hbm, nid_ref), (count_hbm, count_ref), (idx_hbm, idx_ref), (weight_hbm, weight_ref)]
    copies = [pltpu.make_async_copy(a, b, sems.at[i]) for i, (a, b) in enumerate(pairs)]
    for copy in copies:
        copy.start()
    for copy in copies:
        copy.wait()
    rows = STENCIL_ROWS
    stations = idx_ref.shape[0] // 2
    peers = out_ref.shape[0] // rows
    nid = nid_ref[...]
    target = nid // stations
    place = nid % stations
    owners = (iota((peers, stations), 0) == target).astype(F32)
    before = (iota((stations, stations), 0) < iota((stations, stations), 1)).astype(F32)
    earlier = jnp.dot(owners, before, preferred_element_type=F32)
    rank = jnp.sum(owners * earlier, axis=0, keepdims=True)
    same = iota((stations, stations), 0) == iota((stations, stations), 1)
    spread = (iota((stations, LANES), 1) % stations == iota((stations, LANES), 0)).astype(F32)
    wide = jnp.dot(
        jnp.broadcast_to(nid.astype(F32), (peers, stations)),
        spread,
        preferred_element_type=F32,
        precision=HIGHEST,
    )
    lane = iota((peers, LANES), 1)
    places = jnp.full((peers, LANES), -1.0, F32)
    cell = iota((stations, LANES), 1)
    counts = [
        jnp.sum(jnp.where(same, count_ref[azim : azim + 1, :], 0), axis=1, keepdims=True)
        for azim in range(2)
    ]
    for slot in range(SLOTS):
        pick = jnp.where(rank == float(slot), owners, 0.0)
        found = jnp.sum(pick * (place + 1).astype(F32), axis=1, keepdims=True) - 1.0
        places = jnp.where(lane == slot, found, places)
        for azim in range(2):
            idx = idx_ref[pl.ds(azim, stations, stride=2), :]
            live = cell < counts[azim]
            idx = jnp.where(live, idx, -1).astype(F32)
            weight = weight_ref[pl.ds(azim, stations, stride=2), :]
            at = rows_of(slot, azim)
            out_ref[pl.ds(at, peers, stride=rows), :] = jnp.dot(
                pick, idx, preferred_element_type=F32
            )
            out_ref[pl.ds(4 + at, peers, stride=rows), :] = jnp.dot(
                pick, weight, preferred_element_type=F32, precision=HIGHEST
            )
    out_ref[pl.ds(8, peers, stride=rows), :] = wide
    out_ref[pl.ds(9, peers, stride=rows), :] = places


def stencil_place(got_ref, low_ref, up_ref, wl_ref, wu_ref):
    rows = STENCIL_ROWS
    peers = got_ref.shape[0] // rows
    stations = low_ref.shape[0] // 2
    spots = got_ref[pl.ds(9, peers, stride=rows), :].T
    place = iota((stations, peers), 0).astype(F32)
    picks = [jnp.where(spots[slot : slot + 1, :] == place, 1.0, 0.0) for slot in range(SLOTS)]
    for azim in range(2):
        idx = jnp.zeros((stations, LANES), F32)
        weight = jnp.zeros((stations, LANES), F32)
        for slot in range(SLOTS):
            at = rows_of(slot, azim)
            idx += jnp.dot(
                picks[slot],
                got_ref[pl.ds(at, peers, stride=rows), :],
                preferred_element_type=F32,
            )
            weight += jnp.dot(
                picks[slot],
                got_ref[pl.ds(4 + at, peers, stride=rows), :],
                preferred_element_type=F32,
                precision=HIGHEST,
            )
        live = idx >= 0.0
        low = jnp.where(live, idx, 0.0).astype(I32)
        up = low + 1
        here = pl.ds(azim * stations, stations)
        low_ref[here, :] = (low % 4) * 32 + low // 4
        up_ref[here, :] = (up % 4) * 32 + up // 4
        wl_ref[here, :] = jnp.where(live, 1.0 - weight, 0.0)
        wu_ref[here, :] = jnp.where(live, weight, 0.0)


STATE_ROWS = 42


def state_pack(got_ref, x_ref, out_ref, low_ref, up_ref, wl_ref, wu_ref):
    rows, stencil_rows = STATE_ROWS, STENCIL_ROWS
    peers = out_ref.shape[0] // rows
    total = x_ref.shape[1]
    new_rows = got_ref[pl.ds(8, peers, stride=stencil_rows), :].astype(I32)
    quarter = iota((1, LANES), 1) // 32
    tiles = []
    for tile in range(total // LANES):
        row = new_rows[4 * tile : 4 * tile + 1]
        for i in range(1, 4):
            row = jnp.where(quarter == i, new_rows[4 * tile + i : 4 * tile + i + 1], row)
        tiles.append(row)
    nid = jnp.concatenate(tiles, axis=1)
    stations = total // peers
    owner = jnp.broadcast_to((nid // stations).astype(F32), (16, total)).astype(BF16)
    place = jnp.where(iota((stations, total), 0) == nid % stations, 1.0, 0.0).astype(BF16)
    none = jnp.zeros((16, total), BF16)
    high, low = split(x_ref[...])
    both = jnp.concatenate([high, low], axis=0).astype(BF16)
    lines = x_ref.shape[0]
    width = 2 * LANES
    own_cell = iota((8, LANES), 0) % 4 == iota((8, LANES), 1) // 32
    for chunk in range(total // width):
        rows_here = []
        for peer in range(chunk * 8, chunk * 8 + 8):
            mine = owner == jnp.bfloat16(peer)
            rows_here += [
                jnp.where(mine, place[at : at + 16], none) for at in range(0, stations, 16)
            ]
        pick = jnp.concatenate(rows_here, axis=0)
        moved = lax.dot_general(
            both, pick, (((1,), (1,)), ((), ())), preferred_element_type=F32
        )
        moved = moved[:lines] + moved[lines:]
        for tile in range(2):
            y = moved[:, tile * LANES : (tile + 1) * LANES]
            first = (chunk * 2 + tile) * 4
            for group in range(5):
                part = [y[(4 * group + i) * 8 : (4 * group + i + 1) * 8] for i in range(4)]
                turned = []
                for d in range(4):
                    diag = part[d]
                    for q in range(1, 4):
                        diag = jnp.where(quarter == q, part[(q + d) % 4], diag)
                    turned.append(diag if d == 0 else pltpu.roll(diag, 32 * d, 1))
                for q in range(4):
                    out = turned[(-q) % 4]
                    for i in range(1, 4):
                        out = jnp.where(quarter == i, turned[(i - q) % 4], out)
                    at = (first + q) * rows + 8 * group
                    out_ref[at : at + 8, :] = out
            rest = y[160:168]
            turned = [rest] + [pltpu.roll(rest, 32 * d, 1) for d in range(1, 4)]
            for q in range(4):
                out = turned[(-q) % 4]
                for i in range(1, 4):
                    out = jnp.where(quarter == i, turned[(i - q) % 4], out)
                out = jnp.where(own_cell, out, 0.0)
                at = (first + q) * rows + 40
                out_ref[at : at + 1, :] = jnp.sum(out[:4], axis=0, keepdims=True)
                out_ref[at + 1 : at + 2, :] = jnp.sum(out[4:], axis=0, keepdims=True)
    stencil_place(got_ref, low_ref, up_ref, wl_ref, wu_ref)


def line_setup(speed_ref, diffuse_ref, mixing_ref, lines_ref, mix_ref):
    stations = speed_ref.shape[0] // 2
    for azim in range(2):
        here = pl.ds(azim, stations, stride=2)
        lines_ref[pl.ds(azim * stations, stations), :] = speed_ref[here, :]
        lines_ref[pl.ds((2 + azim) * stations, stations), :] = diffuse_ref[here, :]
    nv = mixing_ref.shape[0]
    high, low = split(0.25 * mixing_ref[...])
    by_row = (iota((mix_ref.shape[0], nv), 0) // 8 == iota((mix_ref.shape[0], nv), 1)).astype(F32)
    by_column = (iota((nv, 8 * nv), 0) == iota((nv, 8 * nv), 1) // 8).astype(F32)
    both = [
        jnp.dot(
            jnp.dot(by_row, part, preferred_element_type=F32),
            by_column,
            preferred_element_type=F32,
        )
        for part in (high, low)
    ]
    same = iota(both[0].shape, 0) % 8 == iota(both[0].shape, 1) % 8
    both = [jnp.where(same, part, 0.0) for part in both]
    rest = jnp.zeros((mix_ref.shape[0], mix_ref.shape[1] - 24 * nv), F32)
    mix_ref[...] = jnp.concatenate([both[0], both[0], both[1], rest], axis=1).astype(BF16)


def refit(got_ref, low_ref, up_ref, wl_ref, wu_ref, out_ref, line_ref):
    rows = STATE_ROWS
    stations = low_ref.shape[0] // 2
    nv = out_ref.shape[0] // low_ref.shape[0]

    def lines(first_row):
        cells = [
            got_ref[pl.ds(block * 8 * rows + first_row + c, 8, stride=rows), :]
            for c in range(4)
            for block in range(4)
        ]
        return jnp.concatenate(cells, axis=0).T

    def keep(x, line):
        line_ref[pl.ds(line * stations, stations), :] = x

    for group in range(5):
        for half in range(2):
            x = lines(8 * group + 4 * half)
            for i in range(4):
                keep(x[i * stations : (i + 1) * stations], 8 * group + 2 * i + half)
    lane = iota((stations, LANES), 1)
    last = [got_ref[pl.ds(40 + half, stations, stride=rows), :] for half in range(2)]
    cells = []
    for c in range(4):
        a, b = [
            last[half] if c == half else pltpu.roll(last[half], (32 * (half - c)) % LANES, 1)
            for half in range(2)
        ]
        cells.append(jnp.where(lane < 32, a, b))
    x = jnp.concatenate(cells, axis=0).T
    for half in range(2):
        keep(x[half * stations : (half + 1) * stations], 40 + half)

    def take(x, index):
        return jnp.take_along_axis(x, index, axis=1, mode="promise_in_bounds")

    for azim in range(2):
        for block in range(stations // 8):
            at = azim * stations + 8 * block
            here = pl.ds(at, 8)
            low, up, wl, wu = low_ref[here, :], up_ref[here, :], wl_ref[here, :], wu_ref[here, :]
            parts = [line_ref[pl.ds(2 * stations * v + at, 8), :] for v in range(nv)]
            lower = [wl * take(part, low) for part in parts]
            upper = [wu * take(part, up) for part in parts]
            for v in range(nv):
                fitted = lower[v] + upper[v]
                if v == 0:
                    fitted = jnp.where(wl + wu > 0.0, fitted, MARK)
                out_ref[pl.ds(2 * stations * v + at, 8), :] = fitted


def mixed(mix, fields):
    nv = fields[0].shape[0]
    x = jnp.concatenate([f.reshape(nv * 8, LANES) for f in fields], axis=1)
    high, low = split(x)
    pad = jnp.zeros((mix.shape[1] - 24 * nv, x.shape[1]), F32)
    stacked = jnp.concatenate([high, low, high, pad], axis=0).astype(BF16)
    y = jnp.dot(mix, stacked, preferred_element_type=F32)[: nv * 8]
    return [y[:, i * LANES : (i + 1) * LANES].reshape(nv, 8, LANES) for i in range(len(fields))]


def line_of(ref, azim, block):
    return ref[:, pl.ds(azim * (ref.shape[1] // 2) + 8 * block, 8), :]


def marked_line(ref, azim, block):
    field = line_of(ref, azim, block)
    live = field[:1] < 0.5 * MARK
    first = jnp.where(live, field[:1], 0.0)
    return jnp.concatenate([first, field[1:]], axis=0), jnp.where(live, 1.0, 0.0)


def coefficients(ref, azim, block):
    stations = ref.shape[0] // 4
    return [
        ref[pl.ds((2 * kind + azim) * stations + 8 * block, 8), :][None] for kind in range(2)
    ]


def factors(ref, azim, block, active):
    speed, diffuse = coefficients(ref, azim, block)
    side, below = active * diffuse, active * speed
    own = 1.0 - (2.0 * side + below)
    return own, side, jnp.where(iota(below.shape, 2) == 0, 0.0, below)


def shifted(field):
    return pltpu.roll(field, 1, 2)


def inner(m_ref, lines_ref, mix_ref, base_ref, rest_ref):
    mix = mix_ref[...]
    stations = m_ref.shape[1] // 2
    for block in range(stations // 8):
        field, live = zip(*[marked_line(m_ref, azim, block) for azim in range(2)])
        term = mixed(mix, field)
        base = []
        for azim in range(2):
            own, side, below = factors(lines_ref, azim, block, live[azim])
            base.append(
                (own * field[azim] + side * field[1 - azim])
                + (below * shifted(field[azim]) - live[azim] * term[azim])
            )
        term = mixed(mix, base)
        for azim in range(2):
            here = pl.ds(azim * stations + 8 * block, 8)
            base_ref[:, here, :] = base[azim]
            rest_ref[:, here, :] = 0.5 * (field[azim] - live[azim] * term[azim])


def sections(
    m_ref,
    base_ref,
    rest_ref,
    right_ref,
    left_ref,
    lines_ref,
    lines_left_ref,
    lines_right_ref,
    mix_ref,
    out_hbm,
    out_ref,
    sems,
):
    mix = mix_ref[...]
    stations = m_ref.shape[1] // 2
    copies = []
    for block in range(stations // 8):
        field, live = zip(*[marked_line(m_ref, azim, block) for azim in range(2)])
        near, near_live = zip(
            marked_line(left_ref, 1, block), marked_line(right_ref, 0, block)
        )
        far = [marked_line(left_ref, 0, block)[0], marked_line(right_ref, 1, block)[0]]
        outer = [
            factors(lines_left_ref, 1, block, near_live[0]),
            factors(lines_right_ref, 0, block, near_live[1]),
        ]
        inside = [factors(lines_ref, azim, block, live[azim]) for azim in range(2)]
        near_term = mixed(mix, near)
        first = [
            line_of(base_ref, azim, block) + inside[azim][1] * near[azim] for azim in range(2)
        ]
        for azim in range(2):
            own, side, below = outer[azim]
            beyond = (own * near[azim] + side * (far[azim] + field[azim])) + (
                below * shifted(near[azim]) - near_live[azim] * near_term[azim]
            )
            own, side, below = [0.5 * factor for factor in inside[azim]]
            out = (
                (line_of(rest_ref, azim, block) + own * first[azim])
                + side * ((beyond + first[1 - azim]) - near_term[azim])
                + below * shifted(first[azim])
            )
            out_ref[:, pl.ds(azim + 16 * block, 8, stride=2), :] = out
        done = pl.ds(16 * block, 16)
        copy = pltpu.make_async_copy(
            out_ref.at[:, done, :], out_hbm.at[:, done, :], sems.at[block]
        )
        copy.start()
        copies.append(copy)
    for copy in copies:
        copy.wait()


def shards(
    state_in,
    new_index,
    stencil_index,
    stencil_weight,
    cell_count,
    normal_speed,
    azim_diffusion,
    mixing,
):
    peers = lax.axis_size("stream")
    count = lax.axis_size("azim")
    nv, total, _, cells = state_in.shape
    stations = new_index.shape[0]
    shape = jax.ShapeDtypeStruct

    def flat(a):
        return a.reshape(2 * stations, LANES)

    def exchange(a, rows, tile):
        parts = a.reshape(peers, rows // tile, tile, LANES)
        parts = lax.all_to_all(parts, "stream", split_axis=0, concat_axis=0, tiled=True)
        return parts.reshape(peers * rows, LANES)

    def neighbours(a):
        up = [(i, (i + 1) % count) for i in range(count)]
        down = [((i + 1) % count, i) for i in range(count)]
        return lax.ppermute(a, "azim", up), lax.ppermute(a, "azim", down)

    (packed,) = call(
        stencil_pack,
        [shape((peers * STENCIL_ROWS, LANES), F32)],
        new_index[None],
        flat(stencil_index),
        flat(stencil_weight),
        cell_count.T,
        space=pltpu.HBM,
        scratch=[
            pltpu.VMEM((1, stations), I32),
            pltpu.VMEM((2 * stations, LANES), I32),
            pltpu.VMEM((2 * stations, LANES), F32),
            pltpu.VMEM((2, stations), I32),
            pltpu.SemaphoreType.DMA((4,)),
        ],
        room=60,
    )
    got = exchange(packed, STENCIL_ROWS, 2)

    lines, mix = call(
        line_setup,
        [shape((4 * stations, LANES), F32), shape((8 * nv + 8, 24 * nv + 8), BF16)],
        flat(normal_speed),
        flat(azim_diffusion),
        mixing,
    )
    lines_left, lines_right = neighbours(lines)

    x = state_in.transpose(0, 2, 3, 1).reshape(nv * 2 * cells, total)
    plane = shape((2 * stations, LANES), F32)
    index_plane = shape((2 * stations, LANES), I32)
    packed, low, up, wl, wu = call(
        state_pack,
        [shape((peers * STATE_ROWS, LANES), F32), index_plane, index_plane, plane, plane],
        got,
        x,
    )
    packed, lines_left, lines_right, mix = lax.optimization_barrier(
        (packed, lines_left, lines_right, mix)
    )
    got_state = exchange(packed, STATE_ROWS, 2)

    (moved,) = call(
        refit,
        [shape((nv * 2 * stations, LANES), F32)],
        got_state,
        low,
        up,
        wl,
        wu,
        scratch=[pltpu.VMEM((nv * 2 * stations, LANES), F32)],
    )
    left, right = neighbours(moved)

    field = (nv, 2 * stations, LANES)
    moved = moved.reshape(field)
    base, rest = call(inner, [shape(field, F32)] * 2, moved, lines, mix)
    (out,) = call(
        sections,
        [shape(field, F32)],
        moved,
        base,
        rest,
        right.reshape(field),
        left.reshape(field),
        lines,
        lines_left,
        lines_right,
        mix,
        out_space=pltpu.HBM,
        scratch=[pltpu.VMEM(field, F32), pltpu.SemaphoreType.DMA((4,))],
    )
    return out.reshape(nv, stations, 2, LANES)


def solution(mesh):
    in_specs = (
        P(None, None, "azim", "stream"),
        P("stream"),
        P("stream", "azim", None),
        P("stream", "azim", None),
        P("stream", "azim"),
        P("stream", "azim", None),
        P("stream", "azim", None),
        P(),
    )
    out_specs = P(None, "stream", "azim", None)
    return jax.shard_map(shards, mesh=mesh, in_specs=in_specs, out_specs=out_specs, check_vma=False)
```

```python
import functools
import jax
import jax.numpy as jnp
from jax import lax
from jax.experimental import pallas as pl
from jax.experimental.pallas import tpu as pltpu
from jax.sharding import PartitionSpec as P

LANES = 128
SLOTS = 2
MARK = 1e30
HIGHEST = lax.Precision.HIGHEST
F32 = jnp.float32
BF16 = jnp.bfloat16
I32 = jnp.int32


def call(body, outs, *args, space=pltpu.VMEM, out_space=pltpu.VMEM, scratch=(), room=24):
    touched = sum(a.size * a.dtype.itemsize for a in args) + sum(
        o.dtype.itemsize * functools.reduce(lambda x, y: x * y, o.shape) for o in outs
    )
    return pl.pallas_call(
        body,
        out_shape=outs,
        in_specs=[pl.BlockSpec(memory_space=space)] * len(args),
        out_specs=[pl.BlockSpec(memory_space=out_space)] * len(outs),
        scratch_shapes=list(scratch),
        compiler_params=pltpu.CompilerParams(vmem_limit_bytes=room * 2**20),
        cost_estimate=pl.CostEstimate(flops=0, bytes_accessed=touched, transcendentals=0),
    )(*args)


def iota(shape, dim):
    return lax.broadcasted_iota(I32, shape, dim)


def split(x):
    high = x.astype(BF16).astype(F32)
    return high, x - high


def rows_of(slot, azim):
    return slot * 2 + azim


STENCIL_ROWS = 9


def stencil_pack(nid_hbm, idx_hbm, weight_hbm, count_hbm, out_ref, nid_ref, idx_ref, weight_ref, count_ref, sems):
    pairs = [(nid_hbm, nid_ref), (count_hbm, count_ref), (idx_hbm, idx_ref), (weight_hbm, weight_ref)]
    copies = [pltpu.make_async_copy(a, b, sems.at[i]) for i, (a, b) in enumerate(pairs)]
    for copy in copies:
        copy.start()
    for copy in copies:
        copy.wait()
    rows = STENCIL_ROWS
    stations = idx_ref.shape[0] // 2
    peers = out_ref.shape[0] // rows
    nid = nid_ref[...]
    target = nid // stations
    place = nid % stations
    owners = (iota((peers, stations), 0) == target).astype(F32)
    before = (iota((stations, stations), 0) < iota((stations, stations), 1)).astype(F32)
    earlier = jnp.dot(owners, before, preferred_element_type=F32)
    rank = jnp.sum(owners * earlier, axis=0, keepdims=True)
    same = iota((stations, stations), 0) == iota((stations, stations), 1)
    spread = (iota((stations, LANES), 1) == iota((stations, LANES), 0)).astype(F32)
    wide = jnp.dot(
        jnp.broadcast_to(nid.astype(F32), (peers, stations)),
        spread,
        preferred_element_type=F32,
        precision=HIGHEST,
    )
    lane = iota((peers, LANES), 1)
    places = jnp.full((peers, LANES), -1.0, F32)
    cell = iota((stations, LANES), 1)
    counts = [
        jnp.sum(jnp.where(same, count_ref[azim : azim + 1, :], 0), axis=1, keepdims=True)
        for azim in range(2)
    ]
    for slot in range(SLOTS):
        pick = jnp.where(rank == float(slot), owners, 0.0)
        found = jnp.sum(pick * (place + 1).astype(F32), axis=1, keepdims=True) - 1.0
        places = jnp.where(lane == stations + slot, found, places)
        for azim in range(2):
            idx = idx_ref[pl.ds(azim, stations, stride=2), :]
            live = cell < counts[azim]
            idx = jnp.where(live, idx, -1).astype(F32)
            weight = weight_ref[pl.ds(azim, stations, stride=2), :]
            at = rows_of(slot, azim)
            out_ref[pl.ds(at, peers, stride=rows), :] = jnp.dot(
                pick, idx, preferred_element_type=F32
            )
            out_ref[pl.ds(4 + at, peers, stride=rows), :] = jnp.dot(
                pick, weight, preferred_element_type=F32, precision=HIGHEST
            )
    out_ref[pl.ds(8, peers, stride=rows), :] = jnp.where(lane < stations, wide, places)


def stencil_place(got_ref, low_ref, up_ref, wl_ref, wu_ref):
    rows = STENCIL_ROWS
    peers = got_ref.shape[0] // rows
    stations = low_ref.shape[0] // 2
    spots = got_ref[pl.ds(8, peers, stride=rows), :].T
    place = iota((stations, peers), 0).astype(F32)
    picks = [jnp.where(spots[stations + slot : stations + slot + 1, :] == place, 1.0, 0.0) for slot in range(SLOTS)]
    for azim in range(2):
        idx = jnp.zeros((stations, LANES), F32)
        weight = jnp.zeros((stations, LANES), F32)
        for slot in range(SLOTS):
            at = rows_of(slot, azim)
            idx += jnp.dot(
                picks[slot],
                got_ref[pl.ds(at, peers, stride=rows), :],
                preferred_element_type=F32,
            )
            weight += jnp.dot(
                picks[slot],
                got_ref[pl.ds(4 + at, peers, stride=rows), :],
                preferred_element_type=F32,
                precision=HIGHEST,
            )
        live = idx >= 0.0
        low = jnp.where(live, idx, 0.0).astype(I32)
        up = low + 1
        here = pl.ds(azim * stations, stations)
        low_ref[here, :] = (low % 4) * 32 + low // 4
        up_ref[here, :] = (up % 4) * 32 + up // 4
        wl_ref[here, :] = jnp.where(live, 1.0 - weight, 0.0)
        wu_ref[here, :] = jnp.where(live, weight, 0.0)


STATE_ROWS = 42


def state_pack(got_ref, x_ref, out_ref, low_ref, up_ref, wl_ref, wu_ref):
    rows, stencil_rows = STATE_ROWS, STENCIL_ROWS
    peers = out_ref.shape[0] // rows
    total = x_ref.shape[1]
    new_rows = got_ref[pl.ds(8, peers, stride=stencil_rows), :]
    new_rows = jnp.where(iota((peers, LANES), 1) < 32, new_rows, 0.0)
    new_rows = new_rows + pltpu.roll(new_rows, 64, 1)
    new_rows = (new_rows + pltpu.roll(new_rows, 32, 1)).astype(I32)
    quarter = iota((1, LANES), 1) // 32
    tiles = []
    for tile in range(total // LANES):
        row = new_rows[4 * tile : 4 * tile + 1]
        for i in range(1, 4):
            row = jnp.where(quarter == i, new_rows[4 * tile + i : 4 * tile + i + 1], row)
        tiles.append(row)
    nid = jnp.concatenate(tiles, axis=1)
    stations = total // peers
    owner = jnp.broadcast_to((nid // stations).astype(F32), (16, total)).astype(BF16)
    place = jnp.where(iota((stations, total), 0) == nid % stations, 1.0, 0.0).astype(BF16)
    none = jnp.zeros((16, total), BF16)
    high, low = split(x_ref[...])
    both = jnp.concatenate([high, low], axis=0).astype(BF16)
    lines = x_ref.shape[0]
    width = 2 * LANES
    own_cell = iota((8, LANES), 0) % 4 == iota((8, LANES), 1) // 32
    for chunk in range(total // width):
        rows_here = []
        for peer in range(chunk * 8, chunk * 8 + 8):
            mine = owner == jnp.bfloat16(peer)
            rows_here += [
                jnp.where(mine, place[at : at + 16], none) for at in range(0, stations, 16)
            ]
        pick = jnp.concatenate(rows_here, axis=0)
        moved = lax.dot_general(
            both, pick, (((1,), (1,)), ((), ())), preferred_element_type=F32
        )
        moved = moved[:lines] + moved[lines:]
        for tile in range(2):
            y = moved[:, tile * LANES : (tile + 1) * LANES]
            first = (chunk * 2 + tile) * 4
            for group in range(5):
                part = [y[(4 * group + i) * 8 : (4 * group + i + 1) * 8] for i in range(4)]
                turned = []
                for d in range(4):
                    diag = part[d]
                    for q in range(1, 4):
                        diag = jnp.where(quarter == q, part[(q + d) % 4], diag)
                    turned.append(diag if d == 0 else pltpu.roll(diag, 32 * d, 1))
                for q in range(4):
                    out = turned[(-q) % 4]
                    for i in range(1, 4):
                        out = jnp.where(quarter == i, turned[(i - q) % 4], out)
                    at = (first + q) * rows + 8 * group
                    out_ref[at : at + 8, :] = out
            rest = y[160:168]
            turned = [rest] + [pltpu.roll(rest, 32 * d, 1) for d in range(1, 4)]
            for q in range(4):
                out = turned[(-q) % 4]
                for i in range(1, 4):
                    out = jnp.where(quarter == i, turned[(i - q) % 4], out)
                out = jnp.where(own_cell, out, 0.0)
                at = (first + q) * rows + 40
                out_ref[at : at + 1, :] = jnp.sum(out[:4], axis=0, keepdims=True)
                out_ref[at + 1 : at + 2, :] = jnp.sum(out[4:], axis=0, keepdims=True)
    stencil_place(got_ref, low_ref, up_ref, wl_ref, wu_ref)


def line_setup(speed_ref, diffuse_ref, mixing_ref, lines_ref, mix_ref):
    stations = speed_ref.shape[0] // 2
    for azim in range(2):
        here = pl.ds(azim, stations, stride=2)
        lines_ref[pl.ds(azim * stations, stations), :] = speed_ref[here, :]
        lines_ref[pl.ds((2 + azim) * stations, stations), :] = diffuse_ref[here, :]
    nv = mixing_ref.shape[0]
    high, low = split(0.25 * mixing_ref[...])
    by_row = (iota((mix_ref.shape[0], nv), 0) // 8 == iota((mix_ref.shape[0], nv), 1)).astype(F32)
    by_column = (iota((nv, 8 * nv), 0) == iota((nv, 8 * nv), 1) // 8).astype(F32)
    both = [
        jnp.dot(
            jnp.dot(by_row, part, preferred_element_type=F32),
            by_column,
            preferred_element_type=F32,
        )
        for part in (high, low)
    ]
    same = iota(both[0].shape, 0) % 8 == iota(both[0].shape, 1) % 8
    both = [jnp.where(same, part, 0.0) for part in both]
    rest = jnp.zeros((mix_ref.shape[0], mix_ref.shape[1] - 24 * nv), F32)
    mix_ref[...] = jnp.concatenate([both[0], both[0], both[1], rest], axis=1).astype(BF16)


def refit(got_ref, low_ref, up_ref, wl_ref, wu_ref, out_ref, line_ref):
    rows = STATE_ROWS
    stations = low_ref.shape[0] // 2
    nv = out_ref.shape[0] // low_ref.shape[0]

    def lines(first_row):
        cells = [
            got_ref[pl.ds(block * 8 * rows + first_row + c, 8, stride=rows), :]
            for c in range(4)
            for block in range(4)
        ]
        return jnp.concatenate(cells, axis=0).T

    def keep(x, line):
        line_ref[pl.ds(line * stations, stations), :] = x

    for group in range(5):
        for half in range(2):
            x = lines(8 * group + 4 * half)
            for i in range(4):
                keep(x[i * stations : (i + 1) * stations], 8 * group + 2 * i + half)
    lane = iota((stations, LANES), 1)
    last = [got_ref[pl.ds(40 + half, stations, stride=rows), :] for half in range(2)]
    cells = []
    for c in range(4):
        a, b = [
            last[half] if c == half else pltpu.roll(last[half], (32 * (half - c)) % LANES, 1)
            for half in range(2)
        ]
        cells.append(jnp.where(lane < 32, a, b))
    x = jnp.concatenate(cells, axis=0).T
    for half in range(2):
        keep(x[half * stations : (half + 1) * stations], 40 + half)

    def take(x, index):
        return jnp.take_along_axis(x, index, axis=1, mode="promise_in_bounds")

    for azim in range(2):
        for block in range(stations // 8):
            at = azim * stations + 8 * block
            here = pl.ds(at, 8)
            low, up, wl, wu = low_ref[here, :], up_ref[here, :], wl_ref[here, :], wu_ref[here, :]
            parts = [line_ref[pl.ds(2 * stations * v + at, 8), :] for v in range(nv)]
            lower = [wl * take(part, low) for part in parts]
            upper = [wu * take(part, up) for part in parts]
            for v in range(nv):
                fitted = lower[v] + upper[v]
                if v == 0:
                    fitted = jnp.where(wl + wu > 0.0, fitted, MARK)
                out_ref[pl.ds(2 * stations * v + at, 8), :] = fitted


def mixed(mix, fields):
    nv = fields[0].shape[0]
    x = jnp.concatenate([f.reshape(nv * 8, LANES) for f in fields], axis=1)
    high, low = split(x)
    pad = jnp.zeros((mix.shape[1] - 24 * nv, x.shape[1]), F32)
    stacked = jnp.concatenate([high, low, high, pad], axis=0).astype(BF16)
    y = jnp.dot(mix, stacked, preferred_element_type=F32)[: nv * 8]
    return [y[:, i * LANES : (i + 1) * LANES].reshape(nv, 8, LANES) for i in range(len(fields))]


def line_of(ref, azim, block):
    return ref[:, pl.ds(azim * (ref.shape[1] // 2) + 8 * block, 8), :]


def marked_line(ref, azim, block):
    field = line_of(ref, azim, block)
    live = field[:1] < 0.5 * MARK
    first = jnp.where(live, field[:1], 0.0)
    return jnp.concatenate([first, field[1:]], axis=0), jnp.where(live, 1.0, 0.0)


def coefficients(ref, azim, block):
    stations = ref.shape[0] // 4
    return [
        ref[pl.ds((2 * kind + azim) * stations + 8 * block, 8), :][None] for kind in range(2)
    ]


def factors(ref, azim, block, active):
    speed, diffuse = coefficients(ref, azim, block)
    side, below = active * diffuse, active * speed
    own = 1.0 - (2.0 * side + below)
    return own, side, jnp.where(iota(below.shape, 2) == 0, 0.0, below)


def shifted(field):
    return pltpu.roll(field, 1, 2)


def inner(m_ref, lines_ref, mix_ref, base_ref, rest_ref):
    mix = mix_ref[...]
    stations = m_ref.shape[1] // 2
    for block in range(stations // 8):
        field, live = zip(*[marked_line(m_ref, azim, block) for azim in range(2)])
        term = mixed(mix, field)
        base = []
        for azim in range(2):
            own, side, below = factors(lines_ref, azim, block, live[azim])
            base.append(
                (own * field[azim] + side * field[1 - azim])
                + (below * shifted(field[azim]) - live[azim] * term[azim])
            )
        term = mixed(mix, base)
        for azim in range(2):
            here = pl.ds(azim * stations + 8 * block, 8)
            base_ref[:, here, :] = base[azim]
            rest_ref[:, here, :] = 0.5 * (field[azim] - live[azim] * term[azim])


def sections(
    m_ref,
    base_ref,
    rest_ref,
    right_ref,
    left_ref,
    lines_ref,
    lines_left_ref,
    lines_right_ref,
    mix_ref,
    out_hbm,
    out_ref,
    sems,
):
    mix = mix_ref[...]
    stations = m_ref.shape[1] // 2
    copies = []
    for block in range(stations // 8):
        field, live = zip(*[marked_line(m_ref, azim, block) for azim in range(2)])
        near, near_live = zip(
            marked_line(left_ref, 1, block), marked_line(right_ref, 0, block)
        )
        far = [marked_line(left_ref, 0, block)[0], marked_line(right_ref, 1, block)[0]]
        outer = [
            factors(lines_left_ref, 1, block, near_live[0]),
            factors(lines_right_ref, 0, block, near_live[1]),
        ]
        inside = [factors(lines_ref, azim, block, live[azim]) for azim in range(2)]
        near_term = mixed(mix, near)
        first = [
            line_of(base_ref, azim, block) + inside[azim][1] * near[azim] for azim in range(2)
        ]
        for azim in range(2):
            own, side, below = outer[azim]
            beyond = (own * near[azim] + side * (far[azim] + field[azim])) + (
                below * shifted(near[azim]) - near_live[azim] * near_term[azim]
            )
            own, side, below = [0.5 * factor for factor in inside[azim]]
            out = (
                (line_of(rest_ref, azim, block) + own * first[azim])
                + side * ((beyond + first[1 - azim]) - near_term[azim])
                + below * shifted(first[azim])
            )
            out_ref[:, pl.ds(azim + 16 * block, 8, stride=2), :] = out
        done = pl.ds(16 * block, 16)
        copy = pltpu.make_async_copy(
            out_ref.at[:, done, :], out_hbm.at[:, done, :], sems.at[block]
        )
        copy.start()
        copies.append(copy)
    for copy in copies:
        copy.wait()


def shards(
    state_in,
    new_index,
    stencil_index,
    stencil_weight,
    cell_count,
    normal_speed,
    azim_diffusion,
    mixing,
):
    peers = lax.axis_size("stream")
    count = lax.axis_size("azim")
    nv, total, _, cells = state_in.shape
    stations = new_index.shape[0]
    shape = jax.ShapeDtypeStruct

    def flat(a):
        return a.reshape(2 * stations, LANES)

    def exchange(a, rows, tile):
        parts = a.reshape(peers, rows // tile, tile, LANES)
        parts = lax.all_to_all(parts, "stream", split_axis=0, concat_axis=0, tiled=True)
        return parts.reshape(peers * rows, LANES)

    def neighbours(a):
        up = [(i, (i + 1) % count) for i in range(count)]
        down = [((i + 1) % count, i) for i in range(count)]
        return lax.ppermute(a, "azim", up), lax.ppermute(a, "azim", down)

    (packed,) = call(
        stencil_pack,
        [shape((peers * STENCIL_ROWS, LANES), F32)],
        new_index[None],
        flat(stencil_index),
        flat(stencil_weight),
        cell_count.T,
        space=pltpu.HBM,
        scratch=[
            pltpu.VMEM((1, stations), I32),
            pltpu.VMEM((2 * stations, LANES), I32),
            pltpu.VMEM((2 * stations, LANES), F32),
            pltpu.VMEM((2, stations), I32),
            pltpu.SemaphoreType.DMA((4,)),
        ],
        room=60,
    )
    got = exchange(packed, STENCIL_ROWS, 1)

    lines, mix = call(
        line_setup,
        [shape((4 * stations, LANES), F32), shape((8 * nv + 8, 24 * nv + 8), BF16)],
        flat(normal_speed),
        flat(azim_diffusion),
        mixing,
    )
    lines_left, lines_right = neighbours(lines)

    x = state_in.transpose(0, 2, 3, 1).reshape(nv * 2 * cells, total)
    plane = shape((2 * stations, LANES), F32)
    index_plane = shape((2 * stations, LANES), I32)
    packed, low, up, wl, wu = call(
        state_pack,
        [shape((peers * STATE_ROWS, LANES), F32), index_plane, index_plane, plane, plane],
        got,
        x,
    )
    packed, lines_left, lines_right, mix = lax.optimization_barrier(
        (packed, lines_left, lines_right, mix)
    )
    got_state = exchange(packed, STATE_ROWS, 2)

    (moved,) = call(
        refit,
        [shape((nv * 2 * stations, LANES), F32)],
        got_state,
        low,
        up,
        wl,
        wu,
        scratch=[pltpu.VMEM((nv * 2 * stations, LANES), F32)],
    )
    left, right = neighbours(moved)

    field = (nv, 2 * stations, LANES)
    moved = moved.reshape(field)
    base, rest = call(inner, [shape(field, F32)] * 2, moved, lines, mix)
    (out,) = call(
        sections,
        [shape(field, F32)],
        moved,
        base,
        rest,
        right.reshape(field),
        left.reshape(field),
        lines,
        lines_left,
        lines_right,
        mix,
        out_space=pltpu.HBM,
        scratch=[pltpu.VMEM(field, F32), pltpu.SemaphoreType.DMA((4,))],
    )
    return out.reshape(nv, stations, 2, LANES)


def solution(mesh):
    in_specs = (
        P(None, None, "azim", "stream"),
        P("stream"),
        P("stream", "azim", None),
        P("stream", "azim", None),
        P("stream", "azim"),
        P("stream", "azim", None),
        P("stream", "azim", None),
        P(),
    )
    out_specs = P(None, "stream", "azim", None)
    return jax.shard_map(shards, mesh=mesh, in_specs=in_specs, out_specs=out_specs, check_vma=False)
```

```python
import functools
import jax
import jax.numpy as jnp
from jax import lax
from jax.experimental import pallas as pl
from jax.experimental.pallas import tpu as pltpu
from jax.sharding import PartitionSpec as P

LANES = 128
SLOTS = 2
MARK = 1e30
HIGHEST = lax.Precision.HIGHEST
F32 = jnp.float32
BF16 = jnp.bfloat16
I32 = jnp.int32


def call(body, outs, *args, space=pltpu.VMEM, out_space=pltpu.VMEM, scratch=(), room=24):
    touched = sum(a.size * a.dtype.itemsize for a in args) + sum(
        o.dtype.itemsize * functools.reduce(lambda x, y: x * y, o.shape) for o in outs
    )
    return pl.pallas_call(
        body,
        out_shape=outs,
        in_specs=[pl.BlockSpec(memory_space=space)] * len(args),
        out_specs=[pl.BlockSpec(memory_space=out_space)] * len(outs),
        scratch_shapes=list(scratch),
        compiler_params=pltpu.CompilerParams(vmem_limit_bytes=room * 2**20),
        cost_estimate=pl.CostEstimate(flops=0, bytes_accessed=touched, transcendentals=0),
    )(*args)


def iota(shape, dim):
    return lax.broadcasted_iota(I32, shape, dim)


def split(x):
    high = x.astype(BF16).astype(F32)
    return high, x - high


def rows_of(slot, azim):
    return slot * 2 + azim


STENCIL_ROWS = 9


def stencil_pack(nid_hbm, idx_hbm, weight_hbm, count_hbm, out_ref, nid_ref, idx_ref, weight_ref, count_ref, sems):
    pairs = [(nid_hbm, nid_ref), (count_hbm, count_ref), (idx_hbm, idx_ref), (weight_hbm, weight_ref)]
    copies = [pltpu.make_async_copy(a, b, sems.at[i]) for i, (a, b) in enumerate(pairs)]
    for copy in copies:
        copy.start()
    for copy in copies:
        copy.wait()
    rows = STENCIL_ROWS
    stations = idx_ref.shape[0] // 2
    peers = out_ref.shape[0] // rows
    nid = nid_ref[...]
    target = nid // stations
    place = nid % stations
    owners = (iota((peers, stations), 0) == target).astype(F32)
    before = (iota((stations, stations), 0) < iota((stations, stations), 1)).astype(F32)
    earlier = jnp.dot(owners, before, preferred_element_type=F32)
    rank = jnp.sum(owners * earlier, axis=0, keepdims=True)
    same = iota((stations, stations), 0) == iota((stations, stations), 1)
    spread = (iota((stations, LANES), 1) == iota((stations, LANES), 0)).astype(F32)
    wide = jnp.dot(
        jnp.broadcast_to(nid.astype(F32), (peers, stations)),
        spread,
        preferred_element_type=F32,
        precision=HIGHEST,
    )
    lane = iota((peers, LANES), 1)
    places = jnp.full((peers, LANES), -1.0, F32)
    cell = iota((stations, LANES), 1)
    counts = [
        jnp.sum(jnp.where(same, count_ref[azim : azim + 1, :], 0), axis=1, keepdims=True)
        for azim in range(2)
    ]
    for slot in range(SLOTS):
        pick = jnp.where(rank == float(slot), owners, 0.0)
        found = jnp.sum(pick * (place + 1).astype(F32), axis=1, keepdims=True) - 1.0
        places = jnp.where(lane == stations + slot, found, places)
        for azim in range(2):
            idx = idx_ref[pl.ds(azim, stations, stride=2), :]
            live = cell < counts[azim]
            idx = jnp.where(live, idx, -1).astype(F32)
            weight = weight_ref[pl.ds(azim, stations, stride=2), :]
            at = rows_of(slot, azim)
            out_ref[pl.ds(at, peers, stride=rows), :] = jnp.dot(
                pick, idx, preferred_element_type=F32
            )
            out_ref[pl.ds(4 + at, peers, stride=rows), :] = jnp.dot(
                pick, weight, preferred_element_type=F32, precision=HIGHEST
            )
    out_ref[pl.ds(8, peers, stride=rows), :] = jnp.where(lane < stations, wide, places)


def stencil_place(got_ref, low_ref, up_ref, wl_ref, wu_ref):
    rows = STENCIL_ROWS
    peers = got_ref.shape[0] // rows
    stations = low_ref.shape[0] // 2
    spots = got_ref[pl.ds(8, peers, stride=rows), :].T
    place = iota((stations, peers), 0).astype(F32)
    picks = [jnp.where(spots[stations + slot : stations + slot + 1, :] == place, 1.0, 0.0) for slot in range(SLOTS)]
    for azim in range(2):
        idx = jnp.zeros((stations, LANES), F32)
        weight = jnp.zeros((stations, LANES), F32)
        for slot in range(SLOTS):
            at = rows_of(slot, azim)
            idx += jnp.dot(
                picks[slot],
                got_ref[pl.ds(at, peers, stride=rows), :],
                preferred_element_type=F32,
            )
            weight += jnp.dot(
                picks[slot],
                got_ref[pl.ds(4 + at, peers, stride=rows), :],
                preferred_element_type=F32,
                precision=HIGHEST,
            )
        live = idx >= 0.0
        low = jnp.where(live, idx, 0.0).astype(I32)
        up = low + 1
        here = pl.ds(azim * stations, stations)
        low_ref[here, :] = (low % 4) * 32 + low // 4
        up_ref[here, :] = (up % 4) * 32 + up // 4
        wl_ref[here, :] = jnp.where(live, 1.0 - weight, 0.0)
        wu_ref[here, :] = jnp.where(live, weight, 0.0)


STATE_ROWS = 42


def state_pack(got_ref, x_ref, out_ref, low_ref, up_ref, wl_ref, wu_ref):
    rows, stencil_rows = STATE_ROWS, STENCIL_ROWS
    peers = out_ref.shape[0] // rows
    total = x_ref.shape[1]
    new_rows = got_ref[pl.ds(8, peers, stride=stencil_rows), :].astype(I32)
    quarter = iota((1, LANES), 1) // 32
    turned = [new_rows] + [pltpu.roll(new_rows, 32 * i, 1) for i in range(1, 4)]
    tiles = []
    for tile in range(total // LANES):
        row = turned[0][4 * tile : 4 * tile + 1]
        for i in range(1, 4):
            row = jnp.where(quarter == i, turned[i][4 * tile + i : 4 * tile + i + 1], row)
        tiles.append(row)
    nid = jnp.concatenate(tiles, axis=1)
    stations = total // peers
    owner = jnp.broadcast_to((nid // stations).astype(F32), (16, total)).astype(BF16)
    place = jnp.where(iota((stations, total), 0) == nid % stations, 1.0, 0.0).astype(BF16)
    none = jnp.zeros((16, total), BF16)
    high, low = split(x_ref[...])
    both = jnp.concatenate([high, low], axis=0).astype(BF16)
    lines = x_ref.shape[0]
    width = 2 * LANES
    own_cell = iota((8, LANES), 0) % 4 == iota((8, LANES), 1) // 32
    for chunk in range(total // width):
        rows_here = []
        for peer in range(chunk * 8, chunk * 8 + 8):
            mine = owner == jnp.bfloat16(peer)
            rows_here += [
                jnp.where(mine, place[at : at + 16], none) for at in range(0, stations, 16)
            ]
        pick = jnp.concatenate(rows_here, axis=0)
        moved = lax.dot_general(
            both, pick, (((1,), (1,)), ((), ())), preferred_element_type=F32
        )
        moved = moved[:lines] + moved[lines:]
        for tile in range(2):
            y = moved[:, tile * LANES : (tile + 1) * LANES]
            first = (chunk * 2 + tile) * 4
            for group in range(5):
                part = [y[(4 * group + i) * 8 : (4 * group + i + 1) * 8] for i in range(4)]
                turned = []
                for d in range(4):
                    diag = part[d]
                    for q in range(1, 4):
                        diag = jnp.where(quarter == q, part[(q + d) % 4], diag)
                    turned.append(diag if d == 0 else pltpu.roll(diag, 32 * d, 1))
                for q in range(4):
                    out = turned[(-q) % 4]
                    for i in range(1, 4):
                        out = jnp.where(quarter == i, turned[(i - q) % 4], out)
                    at = (first + q) * rows + 8 * group
                    out_ref[at : at + 8, :] = out
            rest = y[160:168]
            turned = [rest] + [pltpu.roll(rest, 32 * d, 1) for d in range(1, 4)]
            for q in range(4):
                out = turned[(-q) % 4]
                for i in range(1, 4):
                    out = jnp.where(quarter == i, turned[(i - q) % 4], out)
                out = jnp.where(own_cell, out, 0.0)
                at = (first + q) * rows + 40
                out_ref[at : at + 1, :] = jnp.sum(out[:4], axis=0, keepdims=True)
                out_ref[at + 1 : at + 2, :] = jnp.sum(out[4:], axis=0, keepdims=True)
    stencil_place(got_ref, low_ref, up_ref, wl_ref, wu_ref)


def line_setup(speed_ref, diffuse_ref, mixing_ref, lines_ref, first_ref, second_ref, mix_ref):
    stations = speed_ref.shape[0] // 2
    for azim in range(2):
        here = pl.ds(azim, stations, stride=2)
        for ref in (lines_ref, first_ref) if azim == 0 else (lines_ref, second_ref):
            at = azim * 2 * stations if ref is lines_ref else 0
            ref[pl.ds(at, stations), :] = speed_ref[here, :]
            ref[pl.ds(at + stations, stations), :] = diffuse_ref[here, :]
    nv = mixing_ref.shape[0]
    high, low = split(0.25 * mixing_ref[...])
    by_row = (iota((mix_ref.shape[0], nv), 0) // 8 == iota((mix_ref.shape[0], nv), 1)).astype(F32)
    by_column = (iota((nv, 8 * nv), 0) == iota((nv, 8 * nv), 1) // 8).astype(F32)
    both = [
        jnp.dot(
            jnp.dot(by_row, part, preferred_element_type=F32),
            by_column,
            preferred_element_type=F32,
        )
        for part in (high, low)
    ]
    same = iota(both[0].shape, 0) % 8 == iota(both[0].shape, 1) % 8
    both = [jnp.where(same, part, 0.0) for part in both]
    rest = jnp.zeros((mix_ref.shape[0], mix_ref.shape[1] - 24 * nv), F32)
    mix_ref[...] = jnp.concatenate([both[0], both[0], both[1], rest], axis=1).astype(BF16)


def refit(got_ref, low_ref, up_ref, wl_ref, wu_ref, out_ref, line_ref):
    rows = STATE_ROWS
    stations = low_ref.shape[0] // 2
    nv = out_ref.shape[0] // low_ref.shape[0]

    def lines(first_row):
        cells = [
            got_ref[pl.ds(block * 8 * rows + first_row + c, 8, stride=rows), :]
            for c in range(4)
            for block in range(4)
        ]
        return jnp.concatenate(cells, axis=0).T

    def keep(x, line):
        line_ref[pl.ds(line * stations, stations), :] = x

    for group in range(5):
        for half in range(2):
            x = lines(8 * group + 4 * half)
            for i in range(4):
                keep(x[i * stations : (i + 1) * stations], 8 * group + 2 * i + half)
    lane = iota((stations, LANES), 1)
    last = [got_ref[pl.ds(40 + half, stations, stride=rows), :] for half in range(2)]
    cells = []
    for c in range(4):
        a, b = [
            last[half] if c == half else pltpu.roll(last[half], (32 * (half - c)) % LANES, 1)
            for half in range(2)
        ]
        cells.append(jnp.where(lane < 32, a, b))
    x = jnp.concatenate(cells, axis=0).T
    for half in range(2):
        keep(x[half * stations : (half + 1) * stations], 40 + half)

    def take(x, index):
        return jnp.take_along_axis(x, index, axis=1, mode="promise_in_bounds")

    for azim in range(2):
        for block in range(stations // 8):
            at = azim * stations + 8 * block
            here = pl.ds(at, 8)
            low, up, wl, wu = low_ref[here, :], up_ref[here, :], wl_ref[here, :], wu_ref[here, :]
            parts = [line_ref[pl.ds(2 * stations * v + at, 8), :] for v in range(nv)]
            lower = [wl * take(part, low) for part in parts]
            upper = [wu * take(part, up) for part in parts]
            for v in range(nv):
                fitted = lower[v] + upper[v]
                if v == 0:
                    fitted = jnp.where(wl + wu > 0.0, fitted, MARK)
                out_ref[pl.ds(2 * stations * v + at, 8), :] = fitted


def mixed(mix, fields):
    nv = fields[0].shape[0]
    x = jnp.concatenate([f.reshape(nv * 8, LANES) for f in fields], axis=1)
    high, low = split(x)
    pad = jnp.zeros((mix.shape[1] - 24 * nv, x.shape[1]), F32)
    stacked = jnp.concatenate([high, low, high, pad], axis=0).astype(BF16)
    y = jnp.dot(mix, stacked, preferred_element_type=F32)[: nv * 8]
    return [y[:, i * LANES : (i + 1) * LANES].reshape(nv, 8, LANES) for i in range(len(fields))]


def line_of(ref, azim, block):
    return ref[:, pl.ds(azim * (ref.shape[1] // 2) + 8 * block, 8), :]


def marked_line(ref, azim, block):
    field = line_of(ref, azim, block)
    live = field[:1] < 0.5 * MARK
    first = jnp.where(live, field[:1], 0.0)
    return jnp.concatenate([first, field[1:]], axis=0), jnp.where(live, 1.0, 0.0)


def coefficients(ref, azim, block):
    stations = ref.shape[0] // 4 if azim is not None else ref.shape[0] // 2
    return [
        ref[pl.ds((2 * (azim or 0) + kind) * stations + 8 * block, 8), :][None] for kind in range(2)
    ]


def factors(ref, azim, block, active):
    speed, diffuse = coefficients(ref, azim, block)
    side, below = active * diffuse, active * speed
    own = 1.0 - (2.0 * side + below)
    return own, side, jnp.where(iota(below.shape, 2) == 0, 0.0, below)


def shifted(field):
    return pltpu.roll(field, 1, 2)


def inner(m_ref, lines_ref, mix_ref, base_ref, rest_ref):
    mix = mix_ref[...]
    stations = m_ref.shape[1] // 2
    for block in range(stations // 8):
        field, live = zip(*[marked_line(m_ref, azim, block) for azim in range(2)])
        term = mixed(mix, field)
        base = []
        for azim in range(2):
            own, side, below = factors(lines_ref, azim, block, live[azim])
            base.append(
                (own * field[azim] + side * field[1 - azim])
                + (below * shifted(field[azim]) - live[azim] * term[azim])
            )
        term = mixed(mix, base)
        for azim in range(2):
            here = pl.ds(azim * stations + 8 * block, 8)
            base_ref[:, here, :] = base[azim]
            rest_ref[:, here, :] = 0.5 * (field[azim] - live[azim] * term[azim])


def sections(
    lines_right_ref,
    m_ref,
    base_ref,
    rest_ref,
    right_ref,
    left_ref,
    lines_ref,
    lines_left_ref,
    mix_ref,
    out_hbm,
    out_ref,
    sems,
):
    mix = mix_ref[...]
    stations = m_ref.shape[1] // 2
    copies = []
    for block in range(stations // 8):
        field, live = zip(*[marked_line(m_ref, azim, block) for azim in range(2)])
        near, near_live = zip(
            marked_line(left_ref, 1, block), marked_line(right_ref, 0, block)
        )
        far = [marked_line(left_ref, 0, block)[0], marked_line(right_ref, 1, block)[0]]
        outer = [
            factors(lines_left_ref, None, block, near_live[0]),
            factors(lines_right_ref, None, block, near_live[1]),
        ]
        inside = [factors(lines_ref, azim, block, live[azim]) for azim in range(2)]
        near_term = mixed(mix, near)
        first = [
            line_of(base_ref, azim, block) + inside[azim][1] * near[azim] for azim in range(2)
        ]
        for azim in range(2):
            own, side, below = outer[azim]
            beyond = (own * near[azim] + side * (far[azim] + field[azim])) + (
                below * shifted(near[azim]) - near_live[azim] * near_term[azim]
            )
            own, side, below = [0.5 * factor for factor in inside[azim]]
            out = (
                (line_of(rest_ref, azim, block) + own * first[azim])
                + side * ((beyond + first[1 - azim]) - near_term[azim])
                + below * shifted(first[azim])
            )
            out_ref[:, pl.ds(azim + 16 * block, 8, stride=2), :] = out
        done = pl.ds(16 * block, 16)
        copy = pltpu.make_async_copy(
            out_ref.at[:, done, :], out_hbm.at[:, done, :], sems.at[block]
        )
        copy.start()
        copies.append(copy)
    for copy in copies:
        copy.wait()


def shards(
    state_in,
    new_index,
    stencil_index,
    stencil_weight,
    cell_count,
    normal_speed,
    azim_diffusion,
    mixing,
):
    peers = lax.axis_size("stream")
    count = lax.axis_size("azim")
    nv, total, _, cells = state_in.shape
    stations = new_index.shape[0]
    shape = jax.ShapeDtypeStruct

    def flat(a):
        return a.reshape(2 * stations, LANES)

    def exchange(a, rows, tile):
        parts = a.reshape(peers, rows // tile, tile, LANES)
        parts = lax.all_to_all(parts, "stream", split_axis=0, concat_axis=0, tiled=True)
        return parts.reshape(peers * rows, LANES)

    def neighbours(a):
        up = [(i, (i + 1) % count) for i in range(count)]
        down = [((i + 1) % count, i) for i in range(count)]
        return lax.ppermute(a, "azim", up), lax.ppermute(a, "azim", down)

    (packed,) = call(
        stencil_pack,
        [shape((peers * STENCIL_ROWS, LANES), F32)],
        new_index[None],
        flat(stencil_index),
        flat(stencil_weight),
        cell_count.T,
        space=pltpu.HBM,
        scratch=[
            pltpu.VMEM((1, stations), I32),
            pltpu.VMEM((2 * stations, LANES), I32),
            pltpu.VMEM((2 * stations, LANES), F32),
            pltpu.VMEM((2, stations), I32),
            pltpu.SemaphoreType.DMA((4,)),
        ],
        room=60,
    )
    got = exchange(packed, STENCIL_ROWS, 1)

    one = shape((2 * stations, LANES), F32)
    lines, line_first, line_second, mix = call(
        line_setup,
        [shape((4 * stations, LANES), F32), one, one, shape((8 * nv + 8, 24 * nv + 8), BF16)],
        flat(normal_speed),
        flat(azim_diffusion),
        mixing,
    )
    upward = [(i, (i + 1) % count) for i in range(count)]
    lines_left = lax.ppermute(line_second, "azim", upward)

    x = state_in.transpose(0, 2, 3, 1).reshape(nv * 2 * cells, total)
    plane = shape((2 * stations, LANES), F32)
    index_plane = shape((2 * stations, LANES), I32)
    packed, low, up, wl, wu = call(
        state_pack,
        [shape((peers * STATE_ROWS, LANES), F32), index_plane, index_plane, plane, plane],
        got,
        x,
    )
    packed, lines_left, mix = lax.optimization_barrier((packed, lines_left, mix))
    got_state = exchange(packed, STATE_ROWS, 2)

    (moved,) = call(
        refit,
        [shape((nv * 2 * stations, LANES), F32)],
        got_state,
        low,
        up,
        wl,
        wu,
        scratch=[pltpu.VMEM((nv * 2 * stations, LANES), F32)],
    )
    moved, line_first = lax.optimization_barrier((moved, line_first))
    lines_right = lax.ppermute(line_first, "azim", [(j, i) for i, j in upward])
    left, right = neighbours(moved)

    field = (nv, 2 * stations, LANES)
    moved = moved.reshape(field)
    base, rest = call(inner, [shape(field, F32)] * 2, moved, lines, mix)
    (out,) = call(
        sections,
        [shape(field, F32)],
        lines_right,
        moved,
        base,
        rest,
        right.reshape(field),
        left.reshape(field),
        lines,
        lines_left,
        mix,
        out_space=pltpu.HBM,
        scratch=[pltpu.VMEM(field, F32), pltpu.SemaphoreType.DMA((4,))],
    )
    return out.reshape(nv, stations, 2, LANES)


def solution(mesh):
    in_specs = (
        P(None, None, "azim", "stream"),
        P("stream"),
        P("stream", "azim", None),
        P("stream", "azim", None),
        P("stream", "azim"),
        P("stream", "azim", None),
        P("stream", "azim", None),
        P(),
    )
    out_specs = P(None, "stream", "azim", None)
    return jax.shard_map(shards, mesh=mesh, in_specs=in_specs, out_specs=out_specs, check_vma=False)
```
